256 devices in a mesh: grp: 4 (over z_lo, core), tm: 64 (over x, y, z_hi).
Axes of the slice: x: 4, y: 4, z: 8 (z_hi: 4, z_lo: 2; z = z_hi * 2 + z_lo), core: 2. Of those that a mesh axis runs over, the one named last changes fastest.
Arguments:
- seed_field: float32 [4, 2, 8388608], P('grp', None, 'tm'), may hold values from -4 to 4
Outputs:
- spectrogram: float32 [4, 8192, 2048], P('grp', 'tm')
- correlation: float32 [16384, 16384], P('tm', 'grp')
The draws below stay inside these ranges and needn't reach their ends.
All inputs are finite; a program needn't handle non-finite values.
Results may differ from the reference program's by a relative error of at most 0.0003.
Values sent between devices are 32-bit elements; how exact they have to be, the bound alone decides.
No kernel may reach another device: no remote copies, remote signals or barrier semaphores. Data moves between devices by JAX's collectives and lax.ppermute only.
A program may use at most 128 MiB of HBM per device.

```python
import math
import jax
import jax.numpy as jnp
from jax import lax

W = 2048
BINS = 16384
TAPS = 512
NT = 8388608
HOP = 1024
FRAMES = 8192
BIN_WIDTH = 512
REALS = 4
DISP_MOD = 268435456


def steps_of(rng, dims, shards, least, largest):
    loudness, own = 1.0, jax.random.fold_in(rng, 6)
    for axis_at, shards_of in shards:
        heights = jnp.exp(jax.random.uniform(jax.random.fold_in(own, axis_at), (shards_of,), jnp.float32, least / len(shards), largest / len(shards)))
        loudness = loudness * jnp.repeat(heights, dims[axis_at] // shards_of).reshape([-1 if axis == axis_at else 1 for axis in range(len(dims))])
    return loudness


def bell_draw(rng, shape, width, reach, cuts=(), held_as=jnp.bfloat16):
    array = width * jax.random.normal(rng, shape, jnp.float32)
    if cuts:
        array = array * steps_of(rng, shape, cuts, -0.22, 0.18)
    return jnp.clip(array, -reach, reach).astype(held_as)


def setup_inputs(seed: int = 0) -> dict:
    arg_keys = jax.random.split(jax.random.key(seed), 2)
    seed_field = bell_draw(arg_keys[0], (REALS, 2, NT), 0.5, 4.0, ((0, 4), (2, 64)), jnp.float32)
    return {"seed_field": seed_field}


PEAK_AMPLITUDE = 2.0
KERR_GAIN = 0.5
RAMAN_SHARE = 0.18
RESPONSE_FAST = 12.2
RESPONSE_SLOW = 32.0
RESPONSE_SCALE = (12.2 * 12.2 + 32.0 * 32.0) / (12.2 * 32.0 * 32.0)
FLOOR_SHARE = 0.5

def response_taps(position):
    lag_value = position.astype(jnp.float32)
    return RESPONSE_SCALE * jnp.exp(-lag_value / RESPONSE_SLOW) * jnp.sin(lag_value / RESPONSE_FAST)

def dispersion_phase(frequency, modulus):
    residue = frequency * frequency & modulus - 1
    return 2.0 * math.pi / modulus * residue.astype(jnp.float32)

def one_realization(seed_pair):
    sample = jnp.arange(NT, dtype=jnp.int32)
    offset = (sample - NT // 2).astype(jnp.float32) * (16.0 / NT)
    pulse = PEAK_AMPLITUDE / jnp.cosh(offset)
    field_re = pulse + seed_pair[0]
    field_im = seed_pair[1]
    field = lax.complex(field_re, field_im)
    intensity = field_re * field_re + field_im * field_im
    frequency = jnp.where(sample < NT // 2, sample, sample - NT)
    response = jnp.where(sample < TAPS, response_taps(sample), jnp.zeros_like(intensity))
    raman = jnp.real(jnp.fft.ifft(jnp.fft.fft(response) * jnp.fft.fft(intensity)))
    phase = KERR_GAIN * ((1.0 - RAMAN_SHARE) * intensity + RAMAN_SHARE * raman)
    kerr = field * lax.complex(jnp.cos(phase), jnp.sin(phase))
    dispersion = dispersion_phase(frequency, DISP_MOD)
    spectrum = jnp.fft.fft(kerr) * lax.complex(jnp.cos(dispersion), jnp.sin(dispersion))
    power = jnp.real(spectrum) ** 2 + jnp.imag(spectrum) ** 2
    bins = lax.optimization_barrier(jnp.sum(power.reshape(BINS, BIN_WIDTH), axis=1)) / float(NT * BIN_WIDTH)
    output_field = jnp.fft.ifft(spectrum)
    blocks = output_field.reshape(FRAMES, HOP)
    frames = jnp.concatenate([blocks, jnp.roll(blocks, -1, axis=0)], axis=1)
    positions = jnp.arange(W, dtype=jnp.int32).astype(jnp.float32)
    window = jnp.sin(math.pi / W * positions) ** 2
    spectra = jnp.fft.fft(frames * window, axis=1)
    gram = (jnp.real(spectra) ** 2 + jnp.imag(spectra) ** 2) / W
    return (gram, bins)

def normalize(bins):
    average = lax.optimization_barrier(jnp.mean(bins, axis=0))
    centred = bins - average
    floor_level = FLOOR_SHARE * average * average / BIN_WIDTH
    spread = jnp.sqrt(jnp.maximum(lax.optimization_barrier(jnp.mean(centred * centred, axis=0)), floor_level))
    return centred / spread

def reference(seed_field):
    spectrogram, bins = lax.map(one_realization, seed_field)
    normal = normalize(bins)
    correlation = jnp.dot(normal.T, normal, precision=lax.Precision.HIGHEST, preferred_element_type=jnp.float32) / REALS
    return (spectrogram, correlation)
```

```python
import functools
import math

import jax
import jax.numpy as jnp
import ml_dtypes
import numpy as np
from jax import lax
from jax.experimental import pallas as pl
from jax.experimental.pallas import tpu as pltpu
from jax.sharding import PartitionSpec as P

NT = 1 << 23
LOCAL = 1 << 17
HOPS = 128
HOP = 1024
W = 2048
BINS = 16384
TAPS = 512
BIN_WIDTH = 512
PEAK_AMPLITUDE = 2.0
KERR_GAIN = 0.5
RAMAN_SHARE = 0.18
RESPONSE_FAST = 12.2
RESPONSE_SLOW = 32.0
RESPONSE_SCALE = (12.2 * 12.2 + 32.0 * 32.0) / (12.2 * 32.0 * 32.0)
FLOOR_SHARE = 0.5
F32 = jnp.float32
BF16 = jnp.bfloat16
VMEM = pl.BlockSpec(memory_space=pltpu.VMEM)
SMEM = pl.BlockSpec(memory_space=pltpu.SMEM)
PARAMS = pltpu.CompilerParams(vmem_limit_bytes=48 * 1024 * 1024)


def split_const(table):
    table = np.asarray(table, np.float64)
    high = table.astype(ml_dtypes.bfloat16)
    low = (table - high.astype(np.float64)).astype(ml_dtypes.bfloat16)
    return np.stack([high, low])


def left_form(matrix):
    return np.block([[matrix.real, -matrix.imag], [matrix.imag, matrix.real]])


def right_form(matrix):
    return np.block(
        [[matrix.real, matrix.imag], [-matrix.imag, matrix.real]]
    )


def dft(size, sign):
    index = np.arange(size)
    return np.exp(sign * 2j * np.pi * (index[:, None] * index[None, :] % size) / size)


def row_order():
    row = np.arange(256)
    return row // 16 + 16 * (row % 16)


def pair(values):
    return np.stack([values.real, values.imag]).astype(np.float32)


@functools.lru_cache(maxsize=None)
def tables():
    out = {}
    lag = np.arange(256)[None, :] - np.arange(256)[:, None]
    taps = np.arange(TAPS)
    response = RESPONSE_SCALE * np.exp(-taps / RESPONSE_SLOW) * np.sin(taps / RESPONSE_FAST)
    blocks = []
    for step in range(3):
        position = 256 * step + lag
        inside = (position >= 0) & (position < TAPS)
        blocks.append(np.where(inside, response[np.clip(position, 0, TAPS - 1)], 0.0))
    out["toeplitz"] = split_const(np.concatenate(blocks, 0))
    out["hop_fwd"] = split_const(left_form(dft(128, -1)))
    out["sub_fwd"] = split_const(right_form(dft(256, -1)))
    out["sub_inv"] = split_const(left_form(dft(256, 1)[row_order()]) / NT)
    out["hop_inv"] = split_const(right_form(dft(128, 1)))
    hops = np.arange(HOPS)
    for name, span in (("p1", 1 << 23), ("p2", 1 << 21), ("p3", 1 << 19)):
        turn = np.exp(-2j * np.pi * 1024 * hops / span)
        out[name + "_rows"] = pair(np.repeat(turn[:, None], 128, 1))
        out[name + "_lanes"] = pair(np.conj(turn)[None, :])
    sub = np.arange(256)
    turn = np.exp(-2j * np.pi * sub / 1024)
    out["p4_lanes"] = pair(turn[None, :])
    out["p4_rows"] = pair(np.repeat(np.conj(turn)[row_order()][:, None], 128, 1))
    cross = np.exp(-2j * np.pi * np.arange(128)[None, :, None] * (256 * np.arange(4)[:, None, None] + sub) / LOCAL)
    out["cross_fwd"] = np.stack([pair(cross[p]) for p in range(4)])
    out["cross_inv"] = np.stack([pair(np.conj(cross[p]).T[row_order()]) for p in range(4)])
    inner = np.arange(128)
    window = np.sin(np.pi / W * np.arange(W)) ** 2
    frames = []
    for a in range(16):
        block = np.exp(-2j * np.pi * (inner[:, None] * inner[None, :] % 128) / 128)
        block = block * window[a + 16 * inner][None, :]
        block = block * np.exp(-2j * np.pi * a * inner / 2048)[:, None]
        frames.append(left_form(block))
    out["frames"] = split_const(np.stack(frames))
    return out


def halves(value):
    high = value.astype(BF16)
    low = (value - high.astype(F32)).astype(BF16)
    return high, low


def dims(contract):
    return (contract, ((), ()))


NN = ((1,), (0,))
NT_FORM = ((1,), (1,))


def dot_right(value, table, contract=NN):
    high, low = halves(value)
    dot = lambda a, b: lax.dot_general(a, b, dims(contract), preferred_element_type=F32)
    return dot(high, table[0]) + (dot(high, table[1]) + dot(low, table[0]))


def dot_left(table, value, contract=NN):
    high, low = halves(value)
    dot = lambda a, b: lax.dot_general(a, b, dims(contract), preferred_element_type=F32)
    return dot(table[0], high) + (dot(table[1], high) + dot(table[0], low))


def cmul(a, b):
    return (a[0] * b[0] - a[1] * b[1], a[0] * b[1] + a[1] * b[0])


def quad(x, sign):
    s02 = (x[0][0] + x[2][0], x[0][1] + x[2][1])
    d02 = (x[0][0] - x[2][0], x[0][1] - x[2][1])
    s13 = (x[1][0] + x[3][0], x[1][1] + x[3][1])
    d13 = (x[1][0] - x[3][0], x[1][1] - x[3][1])
    turned = (-sign * d13[1], sign * d13[0])
    return [
        (s02[0] + s13[0], s02[1] + s13[1]),
        (d02[0] + turned[0], d02[1] + turned[1]),
        (s02[0] - s13[0], s02[1] - s13[1]),
        (d02[0] - turned[0], d02[1] - turned[1]),
    ]


def powers(first):
    second = (first[0] * first[0] - first[1] * first[1], 2.0 * first[0] * first[1])
    return [None, first, second, cmul(first, second)]


def twist(values, factors):
    return [values[0]] + [cmul(values[k], factors[k]) for k in (1, 2, 3)]


def sincos(x):
    turns = jnp.floor(x * (2.0 / math.pi) + 0.5)
    rest = ((x - turns * 1.5703125) - turns * 4.837512969970703125e-4) - turns * 7.549789948768648e-8
    sq = rest * rest
    sine = rest + rest * sq * (
        -1.6666654611e-1 + sq * (8.3321608736e-3 + sq * -1.9515295891e-4)
    )
    cosine = 1.0 - 0.5 * sq + sq * sq * (
        4.166664568298827e-2 + sq * (-1.388731625493765e-3 + sq * 2.443315711809948e-5)
    )
    part = turns.astype(jnp.int32)
    odd = (part & 1) == 1
    s_val = jnp.where(odd, cosine, sine)
    c_val = jnp.where(odd, sine, cosine)
    s_val = jnp.where((part & 2) == 2, -s_val, s_val)
    c_val = jnp.where(((part + 1) & 2) == 2, -c_val, c_val)
    return s_val, c_val


def pulse_of(position):
    offset = (position - NT // 2).astype(F32) * (16.0 / NT)
    fall = jnp.exp(-jnp.abs(offset))
    return (2.0 * PEAK_AMPLITUDE) * fall / (1.0 + fall * fall)


def take_blocks(where, blocks, scratch, rows):
    for step in range(4):
        scratch[(where - step) & 3, :, rows, :] = blocks[step][:, rows, :]


def give_blocks(scratch, outs, rows):
    for step in range(4):
        outs[step][:, rows, :] = scratch[step, :, rows, :]


def start_kernel(scal, seed, halo, toep, o0, o1, o2, o3, buf, fre, sc_out):
    outs = (o0, o1, o2, o3)
    out_at = scal[1]
    base = scal[2]
    buf[0:8, 512:1024] = jnp.broadcast_to(halo[...], (8, 512))

    def fill(step, carry):
        rows = pl.ds(pl.multiple_of(step * 8, 8), 8)
        row = lax.broadcasted_iota(jnp.int32, (8, 1024), 0) + step * 8
        lane = lax.broadcasted_iota(jnp.int32, (8, 1024), 1)
        value = seed[0, rows, :] + pulse_of(base + row * 1024 + lane)
        other = seed[1, rows, :]
        fre[rows, :] = value
        buf[pl.ds(pl.multiple_of(step * 8 + 8, 8), 8), :] = value * value + other * other
        return carry

    lax.fori_loop(0, 16, fill, 0)
    own = [halves(buf[8:136, 256 * e : 256 * e + 256]) for e in range(4)]
    back = {e: halves(buf[7:135, 256 * e : 256 * e + 256]) for e in (2, 3)}
    for e in range(4):
        total = None
        for step in range(3):
            at = e - step
            high, low = own[at] if at >= 0 else back[at + 4]
            t_high = toep[0, 256 * step : 256 * step + 256, :]
            t_low = toep[1, 256 * step : 256 * step + 256, :]
            term = (
                jnp.dot(high, t_high, preferred_element_type=F32)
                + jnp.dot(high, t_low, preferred_element_type=F32)
                + jnp.dot(low, t_high, preferred_element_type=F32)
            )
            total = term if total is None else total + term
        lanes = slice(256 * e, 256 * e + 256)
        phase = KERR_GAIN * (
            (1.0 - RAMAN_SHARE) * buf[8:136, lanes] + RAMAN_SHARE * total
        )
        sine, cosine = sincos(phase)
        value = fre[:, lanes]
        other = seed[1, :, lanes]
        slot = (e - out_at) & 3
        sc_out[slot, 0] = value * cosine - other * sine
        sc_out[slot, 1] = value * sine + other * cosine
    for step in range(4):
        outs[step][...] = sc_out[step]


def fwd_kernel(scal, r0, r1, r2, r3, rows_t, lanes_t, o0, o1, o2, o3, sc_in, sc_out):
    def body(step, carry):
        rows = pl.ds(pl.multiple_of(step * 8, 8), 8)
        take_blocks(scal[0], (r0, r1, r2, r3), sc_in, rows)
        x = [(sc_in[t, 0, rows, :], sc_in[t, 1, rows, :]) for t in range(4)]
        wide = lambda v: jnp.concatenate([v, v], axis=1)
        row_f = (wide(rows_t[0, rows, :]), wide(rows_t[1, rows, :]))
        first = cmul(row_f, (lanes_t[0], lanes_t[1]))
        y = twist(quad(x, -1.0), powers(first))
        for k in range(4):
            slot = (k - scal[1]) & 3
            sc_out[slot, 0, rows, :] = y[k][0]
            sc_out[slot, 1, rows, :] = y[k][1]
        give_blocks(sc_out, (o0, o1, o2, o3), rows)
        return carry

    lax.fori_loop(0, 16, body, 0)


def hop_kernel(
    scal, r0, r1, r2, r3, rows_t, lanes_t, mat, cross, o0, o1, o2, o3, sc_in, work, sc_out
):
    def body(step, carry):
        rows = pl.ds(pl.multiple_of(step * 8, 8), 8)
        take_blocks(scal[0], (r0, r1, r2, r3), sc_in, rows)
        x = [(sc_in[t, 0, rows, :], sc_in[t, 1, rows, :]) for t in range(4)]
        wide = lambda v: jnp.concatenate([v, v], axis=1)
        row_f = (wide(rows_t[0, rows, :]), wide(rows_t[1, rows, :]))
        first = cmul(row_f, (lanes_t[0], lanes_t[1]))
        y = twist(quad(x, -1.0), powers(first))
        low_rows = pl.ds(pl.multiple_of(step * 8 + 128, 8), 8)
        for k in range(4):
            work[k, rows, :] = y[k][0]
            work[k, low_rows, :] = y[k][1]
        return carry

    lax.fori_loop(0, 16, body, 0)
    for k in range(4):
        got = dot_left(mat, work[k])
        re, im = cmul((got[:128], got[128:]), (cross[0], cross[1]))
        slot = (k - scal[1]) & 3
        sc_out[slot, 0] = re
        sc_out[slot, 1] = im
    for step, out in enumerate((o0, o1, o2, o3)):
        out[...] = sc_out[step]


def spectrum_kernel(
    scal, r0, r1, r2, r3, lanes_t, mat, disp, inv, rows_t,
    o0, o1, o2, o3, bins, sc_in, work, back, sc_out,
):
    def body(step, carry):
        rows = pl.ds(pl.multiple_of(step * 8, 8), 8)
        take_blocks(scal[0], (r0, r1, r2, r3), sc_in, rows)
        x = [(sc_in[t, 0, rows, :], sc_in[t, 1, rows, :]) for t in range(4)]
        y = twist(quad(x, -1.0), powers((lanes_t[0], lanes_t[1])))
        for k in range(4):
            at = pl.ds(pl.multiple_of(step * 8 + 128 * k, 8), 8)
            work[at, 0:256] = y[k][0]
            work[at, 256:512] = y[k][1]
        return carry

    lax.fori_loop(0, 16, body, 0)
    for k in range(4):
        rows = slice(128 * k, 128 * k + 128)
        got = dot_right(work[rows, :], mat)
        re, im = got[:, :256], got[:, 256:]
        power = (re * re + im * im).reshape(16, 8, 256)
        bins[16 * k : 16 * k + 16, :] = jnp.sum(power, axis=1) * (1.0 / (NT * BIN_WIDTH))
        re, im = cmul((re, im), (disp[0, rows, :], disp[1, rows, :]))
        work[rows, 0:256] = re
        work[rows, 256:512] = im
    back[...] = dot_left(inv, work[...], NT_FORM)

    def tail(step, carry):
        rows = pl.ds(pl.multiple_of(step * 8, 8), 8)
        low_rows = pl.ds(pl.multiple_of(step * 8 + 256, 8), 8)
        x = [
            (back[rows, 128 * k : 128 * k + 128], back[low_rows, 128 * k : 128 * k + 128])
            for k in range(4)
        ]
        y = quad(twist(x, powers((rows_t[0, rows, :], rows_t[1, rows, :]))), 1.0)
        for k in range(4):
            slot = (k - scal[1]) & 3
            sc_out[slot, 0, rows, :] = y[k][0]
            sc_out[slot, 1, rows, :] = y[k][1]
        give_blocks(sc_out, (o0, o1, o2, o3), rows)
        return carry

    lax.fori_loop(0, 32, tail, 0)


def unhop_kernel(
    scal, r0, r1, r2, r3, cross, mat, rows_t, lanes_t, o0, o1, o2, o3, sc_in, work, sc_out
):
    def body(step, carry):
        rows = pl.ds(pl.multiple_of(step * 8, 8), 8)
        take_blocks(scal[0], (r0, r1, r2, r3), sc_in, rows)
        factor = (cross[0, rows, :], cross[1, rows, :])
        for k in range(4):
            re, im = cmul((sc_in[k, 0, rows, :], sc_in[k, 1, rows, :]), factor)
            work[k, rows, 0:128] = re
            work[k, rows, 128:256] = im
        return carry

    lax.fori_loop(0, 32, body, 0)
    for k in range(4):
        work[k] = dot_right(work[k], mat)

    def tail(step, carry):
        rows = pl.ds(pl.multiple_of(step * 8, 8), 8)
        first = cmul((rows_t[0, rows, :], rows_t[1, rows, :]), (lanes_t[0], lanes_t[1]))
        x = [(work[k, rows, 0:128], work[k, rows, 128:256]) for k in range(4)]
        y = quad(twist(x, powers(first)), 1.0)
        for k in range(4):
            slot = (k - scal[1]) & 3
            sc_out[slot, 0, rows, :] = y[k][0]
            sc_out[slot, 1, rows, :] = y[k][1]
        give_blocks(sc_out, (o0, o1, o2, o3), rows)
        return carry

    lax.fori_loop(0, 32, tail, 0)


def inv_kernel(scal, r0, r1, r2, r3, rows_t, lanes_t, o0, o1, o2, o3, sc_in, sc_out):
    def body(step, carry):
        rows = pl.ds(pl.multiple_of(step * 8, 8), 8)
        take_blocks(scal[0], (r0, r1, r2, r3), sc_in, rows)
        first = cmul((rows_t[0, rows, :], rows_t[1, rows, :]), (lanes_t[0], lanes_t[1]))
        x = [(sc_in[k, 0, rows, :], sc_in[k, 1, rows, :]) for k in range(4)]
        y = quad(twist(x, powers(first)), 1.0)
        for k in range(4):
            slot = (k - scal[1]) & 3
            sc_out[slot, 0, rows, :] = y[k][0]
            sc_out[slot, 1, rows, :] = y[k][1]
        give_blocks(sc_out, (o0, o1, o2, o3), rows)
        return carry

    lax.fori_loop(0, 32, body, 0)


def frames_kernel(scal, r0, r1, r2, r3, tail, mat, out, sc_in, nxt, got):
    for step, block in enumerate((r0, r1, r2, r3)):
        sc_in[(scal[0] - step) & 3] = block[...]
    columns = tail[...].T
    lane = lax.broadcasted_iota(jnp.int32, (128, 128), 1)
    for p in range(4):
        for part in range(2):
            for half in range(2):
                at = (p * 2 + part) * 2 + half
                rows = slice(128 * half, 128 * half + 128)
                rolled = pltpu.roll(sc_in[p, part, rows, :], 127, 1)
                nxt[p, part, rows, :] = jnp.where(lane == 127, columns[:, at : at + 1], rolled)
    for a in range(16):
        rows = slice(16 * a, 16 * a + 16)
        pieces = []
        for part in range(2):
            pieces += [sc_in[p, part, rows, :] for p in range(4)]
            pieces += [nxt[p, part, rows, :] for p in range(4)]
        got[a] = dot_left(mat.at[:, a], jnp.concatenate(pieces, axis=0))

    def body(step, carry):
        rows = pl.ds(pl.multiple_of(step * 8, 8), 8)
        low_rows = pl.ds(pl.multiple_of(step * 8 + 128, 8), 8)
        inner = []
        for a0 in range(4):
            x = [(got[4 * a1 + a0, rows, :], got[4 * a1 + a0, low_rows, :]) for a1 in range(4)]
            inner.append(quad(x, -1.0))
        for c0 in range(4):
            x = []
            for a0 in range(4):
                value = inner[a0][c0]
                if a0 * c0:
                    angle = -2.0 * math.pi * a0 * c0 / 16
                    value = cmul(value, (math.cos(angle), math.sin(angle)))
                x.append(value)
            for c1, value in enumerate(quad(x, -1.0)):
                got[c0 + 4 * c1, rows, :] = (value[0] * value[0] + value[1] * value[1]) * (1.0 / W)
        return carry

    lax.fori_loop(0, 16, body, 0)
    for c in range(16):
        out[:, 128 * c : 128 * c + 128] = got[c, 0:128, :].T


def call(kernel, outs, scratch, *args, flops=1 << 20):
    specs = [SMEM] + [VMEM] * (len(args) - 1)
    size = sum(int(np.prod(s)) * 4 for s in outs)
    return pl.pallas_call(
        kernel,
        out_shape=[jax.ShapeDtypeStruct(s, F32) for s in outs],
        in_specs=specs,
        out_specs=[VMEM] * len(outs),
        scratch_shapes=[pltpu.VMEM(s, F32) for s in scratch],
        compiler_params=PARAMS,
        cost_estimate=pl.CostEstimate(flops=flops, bytes_accessed=2 * size, transcendentals=0),
    )(*args)


STRIDE = {"x": 16, "y": 4, "z": 1}


def swap_blocks(blocks, axis):
    stride = STRIDE[axis]
    out = [blocks[0]]
    for step in (1, 3, 2):
        pairs = []
        for device in range(64):
            digit = device // stride % 4
            pairs.append((device, device + ((digit + step) % 4 - digit) * stride))
        out.append(lax.ppermute(blocks[step], "tm", pairs))
    return [out[0], out[1], out[3], out[2]]


def unit(numerator, span, sign):
    angle = (sign * 2.0 * math.pi / span) * numerator.astype(F32)
    return jnp.stack([jnp.cos(angle), jnp.sin(angle)])


FWD = (2, 128, 256)
INV = (2, 256, 128)


def on_device(seed_field):
    table = tables()
    tm = lax.axis_index("tm")
    grp = lax.axis_index("grp")
    ix, iy, iz = tm // 16, tm // 4 % 4, tm % 4
    scal = lambda *v: jnp.stack([jnp.asarray(a, jnp.int32) for a in v])

    seed = seed_field.reshape(2, HOPS, HOP)
    last = seed_field[0, :, LOCAL - TAPS :].reshape(8, 128)
    last = lax.ppermute(last, "tm", [(d, (d + 1) % 64) for d in range(64)]).reshape(2, TAPS)
    spots = (tm * LOCAL - TAPS + jnp.arange(TAPS, dtype=jnp.int32)) & (NT - 1)
    halo = ((last[0] + pulse_of(spots)) ** 2 + last[1] ** 2)[None, :]

    blocks = call(
        start_kernel, [FWD] * 4, [(136, 1024), (128, 1024), (4,) + FWD],
        scal(0, ix, tm * LOCAL), seed, halo, table["toeplitz"],
    )
    sub = jnp.arange(256, dtype=jnp.int32)
    base = 256 * ix + sub
    spots1 = iy * (1 << 19) + iz * (1 << 17) + base
    spots2 = iz * (1 << 17) + base
    order = row_order()
    wide = lambda t: jnp.broadcast_to(t[:, order][:, :, None], (2, 256, 128))

    blocks = swap_blocks(blocks, "x")
    blocks = call(
        fwd_kernel, [FWD] * 4, [(4,) + FWD] * 2, scal(ix, iy), *blocks,
        table["p1_rows"], unit(spots1, 1 << 23, -1)[:, None, :],
    )
    blocks = swap_blocks(blocks, "y")
    blocks = call(
        fwd_kernel, [FWD] * 4, [(4,) + FWD] * 2, scal(iy, iz), *blocks,
        table["p2_rows"], unit(spots2, 1 << 21, -1)[:, None, :],
    )
    blocks = swap_blocks(blocks, "z")
    cross = lax.dynamic_index_in_dim(jnp.asarray(table["cross_fwd"]), ix, 0, keepdims=False)
    blocks = call(
        hop_kernel, [FWD] * 4, [(4,) + FWD, (4, 256, 256), (4,) + FWD], scal(iz, ix), *blocks,
        table["p3_rows"], unit(base, 1 << 19, -1)[:, None, :], table["hop_fwd"], cross,
    )
    blocks = swap_blocks(blocks, "x")
    kx, ky, ka = iy, iz, ix
    number = (
        (kx + 4 * ky + 16 * ka)
        + 8192 * jnp.arange(4, dtype=jnp.int32)[:, None, None]
        + 64 * jnp.arange(128, dtype=jnp.int32)[None, :, None]
        + 32768 * sub[None, None, :]
    ).reshape(512, 256)
    freq = jnp.where(number < NT // 2, number, number - NT)
    residue = freq * freq & ((1 << 28) - 1)
    disp = unit(residue, 1 << 28, 1)
    *blocks, bins = call(
        spectrum_kernel, [INV] * 4 + [(64, 256)],
        [(4,) + FWD, (512, 512), (512, 512), (4,) + INV], scal(ix, ix), *blocks,
        table["p4_lanes"], table["sub_fwd"], disp, table["sub_inv"], table["p4_rows"],
    )
    blocks = swap_blocks(blocks, "x")
    cross = lax.dynamic_index_in_dim(jnp.asarray(table["cross_inv"]), ix, 0, keepdims=False)
    blocks = call(
        unhop_kernel, [INV] * 4, [(4,) + INV, (4, 256, 256), (4,) + INV], scal(ix, iz), *blocks,
        cross, table["hop_inv"], wide(unit(base, 1 << 19, 1)), table["p3_lanes"],
    )
    blocks = swap_blocks(blocks, "z")
    blocks = call(
        inv_kernel, [INV] * 4, [(4,) + INV] * 2, scal(iz, iy), *blocks,
        wide(unit(spots2, 1 << 21, 1)), table["p2_lanes"],
    )
    blocks = swap_blocks(blocks, "y")
    blocks = call(
        inv_kernel, [INV] * 4, [(4,) + INV] * 2, scal(iy, ix), *blocks,
        wide(unit(spots1, 1 << 23, 1)), table["p1_lanes"],
    )
    blocks = swap_blocks(blocks, "x")
    first = jnp.stack([b[:, :, 0] for b in blocks])
    first = jnp.stack([lax.dynamic_index_in_dim(first, (ix - p) & 3, 0, False) for p in range(4)])
    tail = lax.ppermute(
        first.reshape(16, 128), "tm", [((d + 1) % 64, d) for d in range(64)]
    )
    spectrogram = call(
        frames_kernel, [(HOPS, W)], [(4,) + INV, (4,) + INV, (16, 256, 128)],
        scal(ix, 0), *blocks, tail, table["frames"],
    )[0]

    parts = bins.T.reshape(64, 256)
    parts = lax.all_to_all(parts, "tm", split_axis=0, concat_axis=0, tiled=True)
    own = jnp.sum(parts, axis=0, keepdims=True)
    ensemble = lax.all_gather(own, "grp", axis=0, tiled=True)
    average = jnp.mean(ensemble, axis=0)
    centred = ensemble - average
    floor_level = FLOOR_SHARE * average * average / BIN_WIDTH
    spread = jnp.sqrt(jnp.maximum(jnp.mean(centred * centred, axis=0), floor_level))
    normal = centred / spread
    pairs = []
    for g in range(4):
        for d in range(64):
            pairs.append((g * 64 + d, d // 16 * 64 + g * 16 + d % 16))
    columns = lax.ppermute(normal.reshape(8, 128), ("grp", "tm"), pairs).reshape(4, 256)
    for axis, digit in (("z", iz), ("y", iy)):
        stride = STRIDE[axis]
        got = [columns]
        for step in (1, 2, 3):
            perm = []
            for d in range(64):
                at = d // stride % 4
                perm.append((d, d + ((at + step) % 4 - at) * stride))
            got.append(lax.ppermute(columns, "tm", perm))
        got = jnp.stack(got)
        got = jnp.stack([lax.dynamic_index_in_dim(got, (digit - t) & 3, 0, False) for t in range(4)])
        columns = jnp.moveaxis(got, 0, 1).reshape(4, -1)
    side = normal.T * 0.25
    correlation = side[:, 0:1] * columns[0:1]
    for r in range(1, 4):
        correlation = correlation + side[:, r : r + 1] * columns[r : r + 1]
    return spectrogram[None], correlation


def solution(mesh):
    return jax.shard_map(
        on_device,
        mesh=mesh,
        in_specs=(P("grp", None, "tm"),),
        out_specs=(P("grp", "tm", None), P("tm", "grp")),
        check_vma=False,
    )
```

```python
import functools
import math

import jax
import jax.numpy as jnp
import ml_dtypes
import numpy as np
from jax import lax
from jax.experimental import pallas as pl
from jax.experimental.pallas import tpu as pltpu
from jax.sharding import PartitionSpec as P

NT = 1 << 23
LOCAL = 1 << 17
HOPS = 128
HOP = 1024
W = 2048
BINS = 16384
TAPS = 512
BIN_WIDTH = 512
PEAK_AMPLITUDE = 2.0
KERR_GAIN = 0.5
RAMAN_SHARE = 0.18
RESPONSE_FAST = 12.2
RESPONSE_SLOW = 32.0
RESPONSE_SCALE = (12.2 * 12.2 + 32.0 * 32.0) / (12.2 * 32.0 * 32.0)
FLOOR_SHARE = 0.5
F32 = jnp.float32
BF16 = jnp.bfloat16
VMEM = pl.BlockSpec(memory_space=pltpu.VMEM)
HBM = pl.BlockSpec(memory_space=pltpu.HBM)
PARAMS = pltpu.CompilerParams(vmem_limit_bytes=48 * 1024 * 1024)


def split_const(table):
    table = np.asarray(table, np.float64)
    high = table.astype(ml_dtypes.bfloat16)
    low = (table - high.astype(np.float64)).astype(ml_dtypes.bfloat16)
    return np.stack([high, low])


def left_form(matrix):
    return np.block([[matrix.real, -matrix.imag], [matrix.imag, matrix.real]])


def right_form(matrix):
    return np.block([[matrix.real, matrix.imag], [-matrix.imag, matrix.real]])


def dft(size, sign):
    index = np.arange(size)
    return np.exp(sign * 2j * np.pi * (index[:, None] * index[None, :] % size) / size)


def row_order():
    row = np.arange(256)
    return row // 16 + 16 * (row % 16)


@functools.lru_cache(maxsize=None)
def tables():
    out = {}
    lag = np.arange(256)[None, :] - np.arange(256)[:, None]
    taps = np.arange(TAPS)
    response = RESPONSE_SCALE * np.exp(-taps / RESPONSE_SLOW) * np.sin(taps / RESPONSE_FAST)
    blocks = []
    for step in range(3):
        position = 256 * step + lag
        inside = (position >= 0) & (position < TAPS)
        blocks.append(np.where(inside, response[np.clip(position, 0, TAPS - 1)], 0.0))
    out["toeplitz"] = split_const(np.concatenate(blocks, 0))
    out["hop_fwd"] = split_const(left_form(dft(128, -1)))
    out["sub_fwd"] = split_const(right_form(dft(256, -1)))
    out["sub_inv"] = split_const(left_form(dft(256, 1)[row_order()]) / NT)
    out["hop_inv"] = split_const(right_form(dft(128, 1)))
    inner = np.arange(128)
    window = np.sin(np.pi / W * np.arange(W)) ** 2
    frames = []
    for a in range(16):
        block = np.exp(-2j * np.pi * (inner[:, None] * inner[None, :] % 128) / 128)
        block = block * window[a + 16 * inner][None, :]
        block = block * np.exp(-2j * np.pi * a * inner / 2048)[:, None]
        frames.append(left_form(block))
    out["frames"] = split_const(np.stack(frames))
    return out


def halves(value):
    high = value.astype(BF16)
    low = (value - high.astype(F32)).astype(BF16)
    return high, low


def dims(contract):
    return (contract, ((), ()))


NN = ((1,), (0,))
NT_FORM = ((1,), (1,))


def dot_right(value, table, contract=NN):
    high, low = halves(value)
    dot = lambda a, b: lax.dot_general(a, b, dims(contract), preferred_element_type=F32)
    return dot(high, table[0]) + (dot(high, table[1]) + dot(low, table[0]))


def dot_left(table, value, contract=NN):
    high, low = halves(value)
    dot = lambda a, b: lax.dot_general(a, b, dims(contract), preferred_element_type=F32)
    return dot(table[0], high) + (dot(table[1], high) + dot(table[0], low))


def cmul(a, b):
    return (a[0] * b[0] - a[1] * b[1], a[0] * b[1] + a[1] * b[0])


def quad(x, sign):
    s02 = (x[0][0] + x[2][0], x[0][1] + x[2][1])
    d02 = (x[0][0] - x[2][0], x[0][1] - x[2][1])
    s13 = (x[1][0] + x[3][0], x[1][1] + x[3][1])
    d13 = (x[1][0] - x[3][0], x[1][1] - x[3][1])
    turned = (-sign * d13[1], sign * d13[0])
    return [
        (s02[0] + s13[0], s02[1] + s13[1]),
        (d02[0] + turned[0], d02[1] + turned[1]),
        (s02[0] - s13[0], s02[1] - s13[1]),
        (d02[0] - turned[0], d02[1] - turned[1]),
    ]


def powers(first):
    second = (first[0] * first[0] - first[1] * first[1], 2.0 * first[0] * first[1])
    return [None, first, second, cmul(first, second)]


def twist(values, factors):
    return [values[0]] + [cmul(values[k], factors[k]) for k in (1, 2, 3)]


def sincos(x):
    turns = jnp.floor(x * (2.0 / math.pi) + 0.5)
    rest = ((x - turns * 1.5703125) - turns * 4.837512969970703125e-4) - turns * 7.549789948768648e-8
    sq = rest * rest
    sine = rest + rest * sq * (
        -1.6666654611e-1 + sq * (8.3321608736e-3 + sq * -1.9515295891e-4)
    )
    cosine = 1.0 - 0.5 * sq + sq * sq * (
        4.166664568298827e-2 + sq * (-1.388731625493765e-3 + sq * 2.443315711809948e-5)
    )
    part = turns.astype(jnp.int32)
    odd = (part & 1) == 1
    s_val = jnp.where(odd, cosine, sine)
    c_val = jnp.where(odd, sine, cosine)
    s_val = jnp.where((part & 2) == 2, -s_val, s_val)
    c_val = jnp.where(((part + 1) & 2) == 2, -c_val, c_val)
    return s_val, c_val


def pulse_of(position):
    offset = (position - NT // 2).astype(F32) * (16.0 / NT)
    fall = jnp.exp(-jnp.abs(offset))
    return (2.0 * PEAK_AMPLITUDE) * fall / (1.0 + fall * fall)


SHIFT = {"x": 4, "y": 2, "z": 0}


def digits():
    tm = lax.axis_index("tm")
    return {axis: (tm >> SHIFT[axis]) & 3 for axis in SHIFT}


def iota(shape, axis):
    return lax.broadcasted_iota(jnp.int32, shape, axis)


def phasor(number, span, sign):
    sine, cosine = sincos((sign * 2.0 * math.pi / span) * number.astype(F32))
    return cosine, sine


def turn(number, span, sign):
    angle = sign * 2.0 * math.pi * number / span
    return math.cos(angle), math.sin(angle)


def span_of(axis, place):
    if axis == "x":
        return 1 << 23, place["y"] * (1 << 19) + place["z"] * (1 << 17) + 256 * place["x"]
    if axis == "y":
        return 1 << 21, place["z"] * (1 << 17) + 256 * place["x"]
    return 1 << 19, 256 * place["x"]


def fwd_first(axis, place):
    span, base = span_of(axis, place)
    first = phasor(base + 1024 * iota((8, 256), 0) + iota((8, 256), 1), span, -1)
    return first, turn(8 * 1024, span, -1)


def inv_first(axis, place):
    span, base = span_of(axis, place)
    first = phasor(base + 16 * iota((8, 128), 0) + 1024 * iota((8, 128), 1), span, 1)
    return first, turn(1, span, 1), turn(128, span, 1)


def eight(start):
    return pl.ds(pl.multiple_of(start, 8), 8)


def start_kernel(seed, halo, toep_hbm, o0, o1, o2, o3, buf, fre, sc_out, toep, sem):
    copy = pltpu.make_async_copy(toep_hbm, toep, sem)
    copy.start()
    place = digits()
    out_at = place["x"]
    base = lax.axis_index("tm") * LOCAL
    buf[0:8, 512:1024] = jnp.broadcast_to(halo[...], (8, 512))

    def fill(step, carry):
        rows = eight(step * 8)
        row = iota((8, 1024), 0) + step * 8
        value = seed[0, rows, :] + pulse_of(base + row * 1024 + iota((8, 1024), 1))
        other = seed[1, rows, :]
        fre[rows, :] = value
        buf[eight(step * 8 + 8), :] = value * value + other * other
        return carry

    lax.fori_loop(0, 16, fill, 0)
    copy.wait()
    own = [halves(buf[8:136, 256 * e : 256 * e + 256]) for e in range(4)]
    back = {e: halves(buf[7:135, 256 * e : 256 * e + 256]) for e in (2, 3)}
    for e in range(4):
        total = None
        for step in range(3):
            at = e - step
            high, low = own[at] if at >= 0 else back[at + 4]
            t_high = toep[0, 256 * step : 256 * step + 256, :]
            t_low = toep[1, 256 * step : 256 * step + 256, :]
            term = (
                jnp.dot(high, t_high, preferred_element_type=F32)
                + jnp.dot(high, t_low, preferred_element_type=F32)
                + jnp.dot(low, t_high, preferred_element_type=F32)
            )
            total = term if total is None else total + term
        lanes = slice(256 * e, 256 * e + 256)
        phase = KERR_GAIN * ((1.0 - RAMAN_SHARE) * buf[8:136, lanes] + RAMAN_SHARE * total)
        sine, cosine = sincos(phase)
        value = fre[:, lanes]
        other = seed[1, :, lanes]
        slot = (e - out_at) & 3
        sc_out[slot, 0] = value * cosine - other * sine
        sc_out[slot, 1] = value * sine + other * cosine
    for step, out in enumerate((o0, o1, o2, o3)):
        out[...] = sc_out[step]


def take_fwd(where, blocks, scratch, rows):
    for step in range(4):
        scratch[(where - step) & 3, :, rows, :] = blocks[step][:, rows, :]
    return [(scratch[t, 0, rows, :], scratch[t, 1, rows, :]) for t in range(4)]


def fwd_kernel(axis, to, r0, r1, r2, r3, o0, o1, o2, o3, sc_in, sc_out):
    place = digits()
    first, forward = fwd_first(axis, place)

    def body(step, factor):
        rows = eight(step * 8)
        x = take_fwd(place[axis], (r0, r1, r2, r3), sc_in, rows)
        y = twist(quad(x, -1.0), powers(factor))
        for k in range(4):
            slot = (k - place[to]) & 3
            sc_out[slot, 0, rows, :] = y[k][0]
            sc_out[slot, 1, rows, :] = y[k][1]
        for j, out in enumerate((o0, o1, o2, o3)):
            out[:, rows, :] = sc_out[j, :, rows, :]
        return cmul(factor, forward)

    lax.fori_loop(0, 16, body, first)


def hop_kernel(r0, r1, r2, r3, mat, o0, o1, o2, o3, sc_in, work, sc_out, cross):
    place = digits()
    first, forward = fwd_first("z", place)
    number = 256 * place["x"] + iota((8, 256), 1)
    cross_first = phasor(iota((8, 256), 0) * number, LOCAL, -1)
    cross_step = phasor(8 * number, LOCAL, -1)

    def body(step, carry):
        factor, other = carry
        rows = eight(step * 8)
        x = take_fwd(place["z"], (r0, r1, r2, r3), sc_in, rows)
        y = twist(quad(x, -1.0), powers(factor))
        for k in range(4):
            work[k, rows, :] = y[k][0]
            work[k, eight(step * 8 + 128), :] = y[k][1]
        cross[0, rows, :] = other[0]
        cross[1, rows, :] = other[1]
        return cmul(factor, forward), cmul(other, cross_step)

    lax.fori_loop(0, 16, body, (first, cross_first))
    for k in range(4):
        got = dot_left(mat, work[k])
        re, im = cmul((got[:128], got[128:]), (cross[0], cross[1]))
        slot = (k - place["x"]) & 3
        sc_out[slot, 0] = re
        sc_out[slot, 1] = im
    for step, out in enumerate((o0, o1, o2, o3)):
        out[...] = sc_out[step]


def give_inv(outs, y, where, scratch, rows, low_rows):
    for k in range(4):
        slot = (k - where) & 3
        scratch[slot, rows, :] = y[k][0]
        scratch[slot, low_rows, :] = y[k][1]
    for j, out in enumerate(outs):
        out[rows, :] = scratch[j, rows, :]
        out[low_rows, :] = scratch[j, low_rows, :]


def spectrum_kernel(
    r0, r1, r2, r3, mat, disp, inv, o0, o1, o2, o3, sc_in, work, back, sc_out, bins, flip, flat
):
    place = digits()
    outs = (o0, o1, o2, o3)
    lanes = phasor(iota((8, 256), 1), 1024, -1)

    def body(step, carry):
        rows = eight(step * 8)
        x = take_fwd(place["x"], (r0, r1, r2, r3), sc_in, rows)
        y = twist(quad(x, -1.0), powers(lanes))
        for k in range(4):
            at = eight(step * 8 + 128 * k)
            work[at, 0:256] = y[k][0]
            work[at, 256:512] = y[k][1]
        return carry

    lax.fori_loop(0, 16, body, 0)
    bins[64:128, :] = jnp.zeros((64, 256), F32)
    for k in range(4):
        rows = slice(128 * k, 128 * k + 128)
        got = dot_right(work[rows, :], mat)
        re, im = got[:, :256], got[:, 256:]
        power = (re * re + im * im).reshape(16, 8, 256)
        bins[16 * k : 16 * k + 16, :] = jnp.sum(power, axis=1) * (1.0 / (NT * BIN_WIDTH))
        re, im = cmul((re, im), (disp[0, rows, :], disp[1, rows, :]))
        work[rows, 0:256] = re
        work[rows, 256:512] = im
    for half in range(2):
        flip[128 * half : 128 * half + 128, :] = bins[:, 128 * half : 128 * half + 128].T
    flat[...] = flip[pl.ds(0, 128, stride=2), :] + pltpu.roll(flip[pl.ds(1, 128, stride=2), :], 64, 1)
    for j, out in enumerate(outs):
        at = pl.multiple_of(((place["x"] + j) & 3) * 32, 32)
        out[512:544, :] = flat[pl.ds(at, 32), :]
    back[...] = dot_left(inv, work[...], NT_FORM)
    first = phasor(16 * iota((8, 128), 0), 1024, 1)
    forward, half_turn = turn(1, 1024, 1), turn(128, 1024, 1)

    def tail(a, factor):
        for half in range(2):
            rows, low_rows = eight(a * 16 + 8 * half), eight(a * 16 + 8 * half + 256)
            x = [
                (back[rows, 128 * k : 128 * k + 128], back[low_rows, 128 * k : 128 * k + 128])
                for k in range(4)
            ]
            now = cmul(factor, half_turn) if half else factor
            y = quad(twist(x, powers(now)), 1.0)
            give_inv(outs, y, place["x"], sc_out, rows, low_rows)
        return cmul(factor, forward)

    lax.fori_loop(0, 16, tail, first)


def take_inv(where, blocks, scratch, rows, low_rows):
    for step in range(4):
        at = (where - step) & 3
        scratch[at, rows, :] = blocks[step][rows, :]
        scratch[at, low_rows, :] = blocks[step][low_rows, :]
    return [(scratch[k, rows, :], scratch[k, low_rows, :]) for k in range(4)]


def bins_on(blocks, outs):
    total = (blocks[0][512:544, :] + blocks[1][512:544, :]) + (
        blocks[2][512:544, :] + blocks[3][512:544, :]
    )
    for out in outs:
        out[512:544, :] = total


def unhop_kernel(r0, r1, r2, r3, mat, o0, o1, o2, o3, sc_in, work, sc_out):
    place = digits()
    blocks, outs = (r0, r1, r2, r3), (o0, o1, o2, o3)
    bins_on(blocks, outs)
    freq = iota((8, 128), 1)
    cross = phasor((256 * place["x"] + 16 * iota((8, 128), 0)) * freq, LOCAL, 1)
    cross_step, cross_half = phasor(freq, LOCAL, 1), phasor(128 * freq, LOCAL, 1)

    def body(a, factor):
        for half in range(2):
            rows, low_rows = eight(a * 16 + 8 * half), eight(a * 16 + 8 * half + 256)
            x = take_inv(place["x"], blocks, sc_in, rows, low_rows)
            now = cmul(factor, cross_half) if half else factor
            for k in range(4):
                re, im = cmul(x[k], now)
                work[k, rows, 0:128] = re
                work[k, rows, 128:256] = im
        return cmul(factor, cross_step)

    lax.fori_loop(0, 16, body, cross)
    for k in range(4):
        work[k] = dot_right(work[k], mat)
    first, forward, half_turn = inv_first("z", place)

    def tail(a, factor):
        for half in range(2):
            rows, low_rows = eight(a * 16 + 8 * half), eight(a * 16 + 8 * half + 256)
            x = [(work[k, rows, 0:128], work[k, rows, 128:256]) for k in range(4)]
            now = cmul(factor, half_turn) if half else factor
            y = quad(twist(x, powers(now)), 1.0)
            give_inv(outs, y, place["z"], sc_out, rows, low_rows)
        return cmul(factor, forward)

    lax.fori_loop(0, 16, tail, first)


def inv_kernel(axis, to, last, *refs):
    blocks, outs, (sc_in, sc_out) = refs[:4], refs[4:8], refs[-2:]
    bins_on(blocks, outs if not last else ())
    if last:
        refs[8][...] = (blocks[0][512:544, :] + blocks[1][512:544, :]) + (
            blocks[2][512:544, :] + blocks[3][512:544, :]
        )
    place = digits()
    first, forward, half_turn = inv_first(to, place)

    def body(a, factor):
        for half in range(2):
            rows, low_rows = eight(a * 16 + 8 * half), eight(a * 16 + 8 * half + 256)
            x = take_inv(place[axis], blocks, sc_in, rows, low_rows)
            now = cmul(factor, half_turn) if half else factor
            y = quad(twist(x, powers(now)), 1.0)
            give_inv(outs, y, place[to], sc_out, rows, low_rows)
        return cmul(factor, forward)

    lax.fori_loop(0, 16, body, first)


def frames_kernel(r0, r1, r2, r3, tail, mat, out, sc_in, nxt, got):
    place = digits()
    for step, block in enumerate((r0, r1, r2, r3)):
        sc_in[(place["x"] - step) & 3] = block[...]
    columns = tail[...].T
    lane = iota((128, 128), 1)
    for step in range(4):
        p = (place["x"] - step) & 3
        for quarter in range(4):
            at = step * 4 + quarter
            rows = slice(128 * quarter, 128 * quarter + 128)
            rolled = pltpu.roll(sc_in[p, rows, :], 127, 1)
            nxt[p, rows, :] = jnp.where(lane == 127, columns[:, at : at + 1], rolled)
    for a in range(16):
        pieces = []
        for part in range(2):
            rows = slice(256 * part + 16 * a, 256 * part + 16 * a + 16)
            pieces += [sc_in[p, rows, :] for p in range(4)]
            pieces += [nxt[p, rows, :] for p in range(4)]
        got[a] = dot_left(mat.at[:, a], jnp.concatenate(pieces, axis=0))

    def body(step, carry):
        rows = eight(step * 8)
        low_rows = eight(step * 8 + 128)
        inner = []
        for a0 in range(4):
            x = [(got[4 * a1 + a0, rows, :], got[4 * a1 + a0, low_rows, :]) for a1 in range(4)]
            inner.append(quad(x, -1.0))
        for c0 in range(4):
            x = []
            for a0 in range(4):
                value = inner[a0][c0]
                if a0 * c0:
                    value = cmul(value, turn(a0 * c0, 16, -1))
                x.append(value)
            for c1, value in enumerate(quad(x, -1.0)):
                got[c0 + 4 * c1, rows, :] = (value[0] * value[0] + value[1] * value[1]) * (1.0 / W)
        return carry

    lax.fori_loop(0, 16, body, 0)
    for c in range(16):
        out[:, 128 * c : 128 * c + 128] = got[c, 0:128, :].T


def normal_kernel(b0, b1, b2, b3, out):
    blocks = [b[...] for b in (b0, b1, b2, b3)]
    total = (blocks[0] + blocks[1]) + (blocks[2] + blocks[3])
    average = total * 0.25
    centred = [b - average for b in blocks]
    sq = [c * c for c in centred]
    variance = ((sq[0] + sq[1]) + (sq[2] + sq[3])) * 0.25
    spread = jnp.sqrt(jnp.maximum(variance, FLOOR_SHARE * average * average / BIN_WIDTH))
    grp = lax.axis_index("grp")
    for step in range(4):
        out[(grp - step) & 3] = centred[step] / spread


def correlation_kernel(own, cols, out, side, pad):
    step = pl.program_id(0)

    @pl.when(step == 0)
    def _():
        at = (lax.axis_index("tm") & 15) * 2
        pad[...] = jnp.zeros((128, 128), F32)
        for r in range(4):
            for half in range(2):
                pad[2 * r + half : 2 * r + half + 1, :] = own[r, pl.ds(at + half, 1), :] * 0.25
        flipped = pad[...].T
        for r in range(4):
            for half in range(2):
                column = flipped[:, 2 * r + half : 2 * r + half + 1]
                side[r, 128 * half : 128 * half + 128, :] = jnp.broadcast_to(column, (128, 128))

    for group in range(4):
        rows = eight(step * 32 + group * 8)
        factors = [side[r, rows, :] for r in range(4)]
        for k in range(32):
            total = factors[0] * cols[0, k : k + 1, :]
            for r in range(1, 4):
                total = total + factors[r] * cols[r, k : k + 1, :]
            out[8 * group : 8 * group + 8, 128 * k : 128 * k + 128] = total


def call(kernel, outs, scratch, *args, flops=1 << 20, specs=None):
    size = sum(int(np.prod(s)) * 4 for s in outs)
    return pl.pallas_call(
        kernel,
        out_shape=[jax.ShapeDtypeStruct(s, F32) for s in outs],
        in_specs=specs or [VMEM] * len(args),
        out_specs=[VMEM] * len(outs),
        scratch_shapes=[pltpu.VMEM(s, F32) if isinstance(s, tuple) else s for s in scratch],
        compiler_params=PARAMS,
        cost_estimate=pl.CostEstimate(flops=flops, bytes_accessed=2 * size, transcendentals=0),
    )(*args)


def ring(axis, step):
    stride = 1 << SHIFT[axis]
    pairs = []
    for device in range(64):
        digit = device // stride % 4
        pairs.append((device, device + ((digit + step) % 4 - digit) * stride))
    return pairs


def swap_blocks(blocks, axis):
    moved = {step: lax.ppermute(blocks[step], "tm", ring(axis, step)) for step in (1, 3, 2)}
    return [blocks[0], moved[1], moved[2], moved[3]]


FWD = (2, 128, 256)
INV = (512, 128)
MORE = (544, 128)


def on_device(seed_field):
    table = tables()
    tm = lax.axis_index("tm")
    ix, iy, iz = tm // 16, tm // 4 % 4, tm % 4

    seed = seed_field.reshape(2, HOPS, HOP)
    last = seed_field[0, :, LOCAL - TAPS :].reshape(8, 128)
    last = lax.ppermute(last, "tm", [(d, (d + 1) % 64) for d in range(64)]).reshape(2, TAPS)
    spots = (tm * LOCAL - TAPS + jnp.arange(TAPS, dtype=jnp.int32)) & (NT - 1)
    halo = ((last[0] + pulse_of(spots)) ** 2 + last[1] ** 2)[None, :]

    blocks = call(
        start_kernel, [FWD] * 4,
        [(136, 1024), (128, 1024), (4,) + FWD, pltpu.VMEM((2, 768, 256), BF16), pltpu.SemaphoreType.DMA],
        seed, halo, table["toeplitz"], specs=[VMEM, VMEM, HBM],
    )
    blocks = swap_blocks(blocks, "x")
    blocks = call(functools.partial(fwd_kernel, "x", "y"), [FWD] * 4, [(4,) + FWD] * 2, *blocks)
    blocks = swap_blocks(blocks, "y")
    blocks = call(functools.partial(fwd_kernel, "y", "z"), [FWD] * 4, [(4,) + FWD] * 2, *blocks)
    blocks = swap_blocks(blocks, "z")
    blocks = call(
        hop_kernel, [FWD] * 4, [(4,) + FWD, (4, 256, 256), (4,) + FWD, FWD], *blocks, table["hop_fwd"]
    )
    blocks = swap_blocks(blocks, "x")
    number = (
        (iy + 4 * iz + 16 * ix)
        + 8192 * jnp.arange(4, dtype=jnp.int32)[:, None, None]
        + 64 * jnp.arange(128, dtype=jnp.int32)[None, :, None]
        + 32768 * jnp.arange(256, dtype=jnp.int32)[None, None, :]
    ).reshape(512, 256)
    freq = jnp.where(number < NT // 2, number, number - NT)
    angle = (2.0 * math.pi / (1 << 28)) * (freq * freq & ((1 << 28) - 1)).astype(F32)
    disp = jnp.stack([jnp.cos(angle), jnp.sin(angle)])
    blocks = call(
        spectrum_kernel, [MORE] * 4,
        [(4,) + FWD, (512, 512), (512, 512), (4,) + INV, (128, 256), (256, 128), (128, 128)],
        *blocks, table["sub_fwd"], disp, table["sub_inv"],
    )
    blocks = swap_blocks(blocks, "x")
    blocks = call(
        unhop_kernel, [MORE] * 4, [(4,) + INV, (4, 256, 256), (4,) + INV], *blocks, table["hop_inv"]
    )
    blocks = swap_blocks(blocks, "z")
    blocks = call(
        functools.partial(inv_kernel, "z", "y", False), [MORE] * 4, [(4,) + INV] * 2, *blocks
    )
    blocks = swap_blocks(blocks, "y")
    *blocks, bins = call(
        functools.partial(inv_kernel, "y", "x", True), [INV] * 4 + [(32, 128)], [(4,) + INV] * 2, *blocks
    )
    sent = blocks
    blocks = swap_blocks(sent, "x")

    edges = jnp.stack([b[:, 0] for b in sent]).reshape(4, 4, 128)
    behind = [(d // 16 * 16 + (d % 16 + 1) % 16, d) for d in range(64)]
    edges = lax.ppermute(edges, "tm", behind)
    edges = jnp.where(tm % 16 == 15, jnp.roll(edges, -1, axis=0), edges)
    tail = jnp.stack(swap_blocks([edges[j] for j in range(4)], "x")).reshape(16, 128)

    alike = [bins] + [
        lax.ppermute(bins, "grp", [(g, (g + step) % 4) for g in range(4)]) for step in (1, 2, 3)
    ]
    normal = call(normal_kernel, [(4, 32, 128)], [], *alike)[0]
    pairs = []
    for g in range(4):
        for d in range(64):
            pairs.append((g * 64 + d, d // 16 * 64 + g * 16 + d % 16))
    columns = lax.ppermute(normal, ("grp", "tm"), pairs)

    spectrogram = call(
        frames_kernel, [(HOPS, W)], [(4,) + INV, (4,) + INV, (16, 256, 128)],
        *blocks, tail, table["frames"],
    )[0]
    correlation = pl.pallas_call(
        correlation_kernel,
        grid=(8,),
        out_shape=jax.ShapeDtypeStruct((256, 4096), F32),
        in_specs=[pl.BlockSpec((4, 32, 128), lambda i: (0, 0, 0))] * 2,
        out_specs=pl.BlockSpec((32, 4096), lambda i: (i, 0)),
        scratch_shapes=[pltpu.VMEM((4, 256, 128), F32), pltpu.VMEM((128, 128), F32)],
        compiler_params=PARAMS,
        cost_estimate=pl.CostEstimate(flops=1 << 23, bytes_accessed=1 << 22, transcendentals=0),
    )(normal, columns)
    return spectrogram[None], correlation


def solution(mesh):
    return jax.shard_map(
        on_device,
        mesh=mesh,
        in_specs=(P("grp", None, "tm"),),
        out_specs=(P("grp", "tm", None), P("tm", "grp")),
        check_vma=False,
    )
```

```python
import functools
import math

import jax
import jax.numpy as jnp
import ml_dtypes
import numpy as np
from jax import lax
from jax.experimental import pallas as pl
from jax.experimental.pallas import tpu as pltpu
from jax.sharding import PartitionSpec as P

NT = 1 << 23
LOCAL = 1 << 17
HOPS = 128
HOP = 1024
W = 2048
BINS = 16384
TAPS = 512
BIN_WIDTH = 512
PEAK_AMPLITUDE = 2.0
KERR_GAIN = 0.5
RAMAN_SHARE = 0.18
RESPONSE_FAST = 12.2
RESPONSE_SLOW = 32.0
RESPONSE_SCALE = (12.2 * 12.2 + 32.0 * 32.0) / (12.2 * 32.0 * 32.0)
FLOOR_SHARE = 0.5
F32 = jnp.float32
BF16 = jnp.bfloat16
VMEM = pl.BlockSpec(memory_space=pltpu.VMEM)
HBM = pl.BlockSpec(memory_space=pltpu.HBM)
PARAMS = pltpu.CompilerParams(vmem_limit_bytes=48 * 1024 * 1024)


def split_const(table):
    table = np.asarray(table, np.float64)
    high = table.astype(ml_dtypes.bfloat16)
    low = (table - high.astype(np.float64)).astype(ml_dtypes.bfloat16)
    return np.stack([high, low])


def left_form(matrix):
    return np.block([[matrix.real, -matrix.imag], [matrix.imag, matrix.real]])


def right_form(matrix):
    return np.block([[matrix.real, matrix.imag], [-matrix.imag, matrix.real]])


def dft(size, sign):
    index = np.arange(size)
    return np.exp(sign * 2j * np.pi * (index[:, None] * index[None, :] % size) / size)


def row_order():
    row = np.arange(256)
    return row // 16 + 16 * (row % 16)


@functools.lru_cache(maxsize=None)
def tables():
    out = {}
    lag = np.arange(256)[None, :] - np.arange(256)[:, None]
    taps = np.arange(TAPS)
    response = RESPONSE_SCALE * np.exp(-taps / RESPONSE_SLOW) * np.sin(taps / RESPONSE_FAST)
    blocks = []
    for step in range(3):
        position = 256 * step + lag
        inside = (position >= 0) & (position < TAPS)
        blocks.append(np.where(inside, response[np.clip(position, 0, TAPS - 1)], 0.0))
    out["toeplitz"] = split_const(np.concatenate(blocks, 0))
    rows = np.arange(256).reshape(2, 16, 8).transpose(1, 0, 2).reshape(256)
    out["hop_fwd"] = split_const(left_form(dft(128, -1))[:, rows])
    cross = np.exp(-2j * np.pi * np.arange(128)[:, None] * np.arange(1024)[None, :] / LOCAL)
    out["cross"] = np.stack([cross.real, cross.imag]).astype(np.float32)
    out["sub_fwd"] = split_const(right_form(dft(256, -1)))
    out["sub_inv"] = split_const(left_form(dft(256, 1)[row_order()]) / NT)
    out["hop_inv"] = split_const(right_form(dft(128, 1)))
    order = np.arange(256).reshape(2, 2, 64).transpose(1, 0, 2).reshape(256)
    inner = np.arange(128)
    window = np.sin(np.pi / W * np.arange(W)) ** 2
    frames = []
    for a in range(16):
        block = np.exp(-2j * np.pi * (inner[:, None] * inner[None, :] % 128) / 128)
        block = block * window[a + 16 * inner][None, :]
        block = block * np.exp(-2j * np.pi * a * inner / 2048)[:, None]
        frames.append(left_form(block)[:, order])
    out["frames"] = split_const(np.stack(frames))
    return out


def halves(value):
    high = value.astype(BF16)
    low = (value - high.astype(F32)).astype(BF16)
    return high, low


def dims(contract):
    return (contract, ((), ()))


NN = ((1,), (0,))
NT_FORM = ((1,), (1,))


def dot_right(value, table, contract=NN):
    high, low = halves(value)
    dot = lambda a, b: lax.dot_general(a, b, dims(contract), preferred_element_type=F32)
    return dot(high, table[0]) + (dot(high, table[1]) + dot(low, table[0]))


def dot_left(table, value, contract=NN):
    high, low = halves(value)
    dot = lambda a, b: lax.dot_general(a, b, dims(contract), preferred_element_type=F32)
    return dot(table[0], high) + (dot(table[1], high) + dot(table[0], low))


def cmul(a, b):
    return (a[0] * b[0] - a[1] * b[1], a[0] * b[1] + a[1] * b[0])


def quad(x, sign):
    s02 = (x[0][0] + x[2][0], x[0][1] + x[2][1])
    d02 = (x[0][0] - x[2][0], x[0][1] - x[2][1])
    s13 = (x[1][0] + x[3][0], x[1][1] + x[3][1])
    d13 = (x[1][0] - x[3][0], x[1][1] - x[3][1])
    turned = (-sign * d13[1], sign * d13[0])
    return [
        (s02[0] + s13[0], s02[1] + s13[1]),
        (d02[0] + turned[0], d02[1] + turned[1]),
        (s02[0] - s13[0], s02[1] - s13[1]),
        (d02[0] - turned[0], d02[1] - turned[1]),
    ]


def powers(first):
    second = (first[0] * first[0] - first[1] * first[1], 2.0 * first[0] * first[1])
    return [None, first, second, cmul(first, second)]


def twist(values, factors):
    return [values[0]] + [cmul(values[k], factors[k]) for k in (1, 2, 3)]


def sincos(x):
    turns = jnp.floor(x * (2.0 / math.pi) + 0.5)
    rest = ((x - turns * 1.5703125) - turns * 4.837512969970703125e-4) - turns * 7.549789948768648e-8
    sq = rest * rest
    sine = rest + rest * sq * (
        -1.6666654611e-1 + sq * (8.3321608736e-3 + sq * -1.9515295891e-4)
    )
    cosine = 1.0 - 0.5 * sq + sq * sq * (
        4.166664568298827e-2 + sq * (-1.388731625493765e-3 + sq * 2.443315711809948e-5)
    )
    part = turns.astype(jnp.int32)
    odd = (part & 1) == 1
    s_val = jnp.where(odd, cosine, sine)
    c_val = jnp.where(odd, sine, cosine)
    s_val = jnp.where((part & 2) == 2, -s_val, s_val)
    c_val = jnp.where(((part + 1) & 2) == 2, -c_val, c_val)
    return s_val, c_val


def pulse_of(position):
    offset = (position - NT // 2).astype(F32) * (16.0 / NT)
    fall = jnp.exp(-jnp.abs(offset))
    return (2.0 * PEAK_AMPLITUDE) * fall / (1.0 + fall * fall)


SHIFT = {"x": 4, "y": 2, "z": 0}


def digits():
    tm = lax.axis_index("tm")
    return {axis: (tm >> SHIFT[axis]) & 3 for axis in SHIFT}


def iota(shape, axis):
    return lax.broadcasted_iota(jnp.int32, shape, axis)


def phasor(number, span, sign):
    sine, cosine = sincos((sign * 2.0 * math.pi / span) * number.astype(F32))
    return cosine, sine


def turn(number, span, sign):
    angle = sign * 2.0 * math.pi * number / span
    return math.cos(angle), math.sin(angle)


def eight(start):
    return pl.ds(pl.multiple_of(start, 8), 8)


def start_kernel(seed, halo, toep_hbm, out, buf, fre, toep, sem):
    copy = pltpu.make_async_copy(toep_hbm, toep, sem)
    copy.start()
    base = lax.axis_index("tm") * LOCAL
    buf[0:8, 512:1024] = jnp.broadcast_to(halo[...], (8, 512))

    def fill(step, carry):
        rows = eight(step * 8)
        row = iota((8, 1024), 0) + step * 8
        value = seed[0, rows, :] + pulse_of(base + row * 1024 + iota((8, 1024), 1))
        other = seed[1, rows, :]
        fre[rows, :] = value
        buf[eight(step * 8 + 8), :] = value * value + other * other
        return carry

    lax.fori_loop(0, 16, fill, 0)
    copy.wait()
    own = [halves(buf[8:136, 256 * e : 256 * e + 256]) for e in range(4)]
    back = {e: halves(buf[7:135, 256 * e : 256 * e + 256]) for e in (2, 3)}
    for e in range(4):
        total = None
        for step in range(3):
            at = e - step
            high, low = own[at] if at >= 0 else back[at + 4]
            t_high = toep[0, 256 * step : 256 * step + 256, :]
            t_low = toep[1, 256 * step : 256 * step + 256, :]
            term = (
                jnp.dot(high, t_high, preferred_element_type=F32)
                + jnp.dot(high, t_low, preferred_element_type=F32)
                + jnp.dot(low, t_high, preferred_element_type=F32)
            )
            total = term if total is None else total + term
        lanes = slice(256 * e, 256 * e + 256)
        phase = KERR_GAIN * ((1.0 - RAMAN_SHARE) * buf[8:136, lanes] + RAMAN_SHARE * total)
        sine, cosine = sincos(phase)
        value = fre[:, lanes]
        other = seed[1, :, lanes]
        out[:, 0:8, lanes] = (value * cosine - other * sine).reshape(16, 8, 256)
        out[:, 8:16, lanes] = (value * sine + other * cosine).reshape(16, 8, 256)


def sixteen(x, sign):
    inner = [quad([x[4 * a1 + a0] for a1 in range(4)], sign) for a0 in range(4)]
    out = []
    for c0 in range(4):
        row = [inner[a0][c0] for a0 in range(4)]
        row = [cmul(v, turn(a0 * c0, 16, sign)) if a0 * c0 else v for a0, v in enumerate(row)]
        out.append(quad(row, sign))
    return out


def many_powers(first):
    out = [None, first]
    for k in range(2, 16):
        out.append(cmul(out[k // 2], out[k - k // 2]))
    return out


def lanes_at(step):
    return pl.ds(pl.multiple_of(step * 128, 128), 128)


def fwd_kernel(blocks, o0, o1, o2, o3, scratch):
    place = digits()
    block = 4 * place["x"] + place["y"]
    number = place["z"] * LOCAL + (8 * block + iota((8, 128), 0)) * 1024 + iota((8, 128), 1)
    forward = turn(128, NT, -1)

    def body(step, factor):
        lanes = lanes_at(step)
        y = sixteen([(blocks[t, 0:8, lanes], blocks[t, 8:16, lanes]) for t in range(16)], -1.0)
        factors = many_powers(factor)
        for c0 in range(4):
            slot = (c0 - place["z"]) & 3
            for c1 in range(4):
                value = y[c0][c1]
                if c0 + c1:
                    value = cmul(value, factors[c0 + 4 * c1])
                scratch[slot, c1, 0:8, lanes] = value[0]
                scratch[slot, c1, 8:16, lanes] = value[1]
        for j, out in enumerate((o0, o1, o2, o3)):
            out[:, :, lanes] = scratch[j, :, :, lanes]
        return cmul(factor, forward)

    lax.fori_loop(0, 8, body, phasor(number, NT, -1))


def mid_kernel(r0, r1, r2, r3, out):
    place = digits()
    block = 4 * place["x"] + place["y"]
    number = (8 * block + iota((8, 128), 0)) * 1024 + iota((8, 128), 1) + place["z"] * LOCAL
    forward = turn(128, 4 * LOCAL, -1)

    def body(step, factor):
        lanes = lanes_at(step)
        factors = powers(factor)
        for kk in range(4):
            x = [(r[kk, 0:8, lanes], r[kk, 8:16, lanes]) for r in (r0, r1, r2, r3)]
            for ka, value in enumerate(twist(quad(x, 1.0), factors)):
                out[4 * ka + kk, 0:8, lanes] = value[0]
                out[4 * ka + kk, 8:16, lanes] = value[1]
        return cmul(factor, forward)

    lax.fori_loop(0, 8, body, phasor(number, 4 * LOCAL, -1))


def spectrum_kernel(
    blocks, hop, cross, mat, disp, inv, unhop, out, wide, work, back, rows_w, bins, flip, flat
):
    for part in range(4):
        lanes = slice(256 * part, 256 * part + 256)
        wide[:, lanes] = dot_left(hop, blocks[:, :, lanes].reshape(256, 256))
    lane_f = powers(phasor(iota((8, 256), 1), 1024, -1))

    def body(step, carry):
        rows, low_rows = eight(step * 8), eight(step * 8 + 128)
        x = []
        for part in range(4):
            lanes = slice(256 * part, 256 * part + 256)
            factor = (cross[0, rows, lanes], cross[1, rows, lanes])
            x.append(cmul((wide[rows, lanes], wide[low_rows, lanes]), factor))
        y = twist(quad(x, -1.0), lane_f)
        for k in range(4):
            at = eight(step * 8 + 128 * k)
            work[at, 0:256] = y[k][0]
            work[at, 256:512] = y[k][1]
        return carry

    lax.fori_loop(0, 16, body, 0)
    bins[64:128, :] = jnp.zeros((64, 256), F32)
    for k in range(4):
        rows = slice(128 * k, 128 * k + 128)
        got = dot_right(work[rows, :], mat)
        re, im = got[:, :256], got[:, 256:]
        power = (re * re + im * im).reshape(16, 8, 256)
        bins[16 * k : 16 * k + 16, :] = jnp.sum(power, axis=1) * (1.0 / (NT * BIN_WIDTH))
        re, im = cmul((re, im), (disp[0, rows, :], disp[1, rows, :]))
        work[rows, 0:256] = re
        work[rows, 256:512] = im
    for half in range(2):
        flip[128 * half : 128 * half + 128, :] = bins[:, 128 * half : 128 * half + 128].T
    flat[...] = flip[pl.ds(0, 128, stride=2), :] + pltpu.roll(flip[pl.ds(1, 128, stride=2), :], 64, 1)
    for dest in range(16):
        out[dest, 128:136, :] = flat[8 * dest : 8 * dest + 8, :]
    back[...] = dot_left(inv, work[...], NT_FORM)
    first = phasor(16 * iota((8, 128), 0), 1024, 1)
    forward, half_turn = turn(1, 1024, 1), turn(128, 1024, 1)
    freq = iota((8, 128), 1)
    cross_first = phasor(16 * iota((8, 128), 0) * freq, LOCAL, 1)
    cross_step, cross_half = phasor(freq, LOCAL, 1), phasor(128 * freq, LOCAL, 1)
    cross_part = powers(phasor(256 * freq, LOCAL, 1))

    def tail(a, carry):
        factor, other = carry
        for half in range(2):
            rows, low_rows = eight(a * 16 + 8 * half), eight(a * 16 + 8 * half + 256)
            x = [
                (back[rows, 128 * k : 128 * k + 128], back[low_rows, 128 * k : 128 * k + 128])
                for k in range(4)
            ]
            now = cmul(factor, half_turn) if half else factor
            after = cmul(other, cross_half) if half else other
            y = twist(quad(twist(x, powers(now)), 1.0), cross_part)
            for part in range(4):
                value = cmul(y[part], after)
                at = eight(a * 64 + part * 16 + 8 * half)
                rows_w[at, 0:128] = value[0]
                rows_w[at, 128:256] = value[1]
        return cmul(factor, forward), cmul(other, cross_step)

    lax.fori_loop(0, 16, tail, (first, cross_first))
    for part in range(4):
        got = dot_right(rows_w[256 * part : 256 * part + 256, :], unhop)
        for a in range(4):
            out[4 * part + a, 0:64, :] = got[64 * a : 64 * a + 64, 0:128]
            out[4 * part + a, 64:128, :] = got[64 * a : 64 * a + 64, 128:256]


def unmid_kernel(blocks, o0, o1, o2, o3):
    place = digits()
    outs = (o0, o1, o2, o3)
    total = blocks[0, 128:136, :]
    for k in range(1, 16):
        total = total + blocks[k, 128:136, :]
    for out in outs:
        out[512:520, :] = total
    block = 4 * place["x"] + place["y"]
    number = block + 16 * iota((8, 128), 0) + 1024 * iota((8, 128), 1) + place["z"] * LOCAL
    forward = turn(128, 4 * LOCAL, 1)

    def body(step, factor):
        rows, low_rows = eight(step * 8), eight(step * 8 + 64)
        factors = powers(factor)
        for kk in range(4):
            x = [(blocks[4 * ka + kk, rows, :], blocks[4 * ka + kk, low_rows, :]) for ka in range(4)]
            for out, value in zip(outs, quad(twist(x, factors), 1.0)):
                out[eight(step * 8 + 128 * kk), :] = value[0]
                out[eight(step * 8 + 128 * kk + 64), :] = value[1]
        return cmul(factor, forward)

    lax.fori_loop(0, 8, body, phasor(number, 4 * LOCAL, 1))


def inv_kernel(r0, r1, r2, r3, out, bins, scratch):
    place = digits()
    blocks = (r0, r1, r2, r3)
    bins[...] = (r0[512:520, :] + r1[512:520, :]) + (r2[512:520, :] + r3[512:520, :])
    block = 4 * place["x"] + place["y"]
    number = place["z"] * LOCAL + block + 16 * iota((8, 128), 0) + 1024 * iota((8, 128), 1)
    forward = turn(128, NT, 1)

    def body(step, factor):
        for kk in range(4):
            for low in (128 * kk, 128 * kk + 64):
                rows = eight(step * 8 + low)
                for s in range(4):
                    scratch[(place["z"] - s) & 3, rows, :] = blocks[s][rows, :]
        factors = many_powers(factor)
        x = [None] * 16
        for c0 in range(4):
            for c1 in range(4):
                value = (
                    scratch[c0, eight(step * 8 + 128 * c1), :],
                    scratch[c0, eight(step * 8 + 128 * c1 + 64), :],
                )
                x[4 * c1 + c0] = cmul(value, factors[c0 + 4 * c1]) if c0 + c1 else value
        y = sixteen(x, 1.0)
        for a0 in range(4):
            for a1 in range(4):
                out[4 * a1 + a0, eight(step * 8), :] = y[a0][a1][0]
                out[4 * a1 + a0, eight(step * 8 + 64), :] = y[a0][a1][1]
        return cmul(factor, forward)

    lax.fori_loop(0, 8, body, phasor(number, NT, 1))


def frames_kernel(blocks, tail, mat, out, got):
    columns = tail[...].T
    lane = iota((128, 128), 1)
    for a in range(16):
        here = blocks[a]
        after = jnp.where(lane == 127, columns[:, a : a + 1], pltpu.roll(here, 127, 1))
        got[a] = dot_left(mat.at[:, a], jnp.concatenate([here, after], axis=0))

    def body(step, carry):
        rows, low_rows = eight(step * 8), eight(step * 8 + 128)
        y = sixteen([(got[a, rows, :], got[a, low_rows, :]) for a in range(16)], -1.0)
        for c0 in range(4):
            for c1 in range(4):
                value = y[c0][c1]
                got[c0 + 4 * c1, rows, :] = (value[0] * value[0] + value[1] * value[1]) * (1.0 / W)
        return carry

    lax.fori_loop(0, 16, body, 0)
    for c in range(16):
        out[:, 128 * c : 128 * c + 128] = got[c, 0:128, :].T


def normal_kernel(b0, b1, b2, b3, out):
    blocks = [b[...] for b in (b0, b1, b2, b3)]
    total = (blocks[0] + blocks[1]) + (blocks[2] + blocks[3])
    average = total * 0.25
    centred = [b - average for b in blocks]
    sq = [c * c for c in centred]
    variance = ((sq[0] + sq[1]) + (sq[2] + sq[3])) * 0.25
    spread = jnp.sqrt(jnp.maximum(variance, FLOOR_SHARE * average * average / BIN_WIDTH))
    grp = lax.axis_index("grp")
    for step in range(4):
        out[(grp - step) & 3] = centred[step] / spread


def correlation_kernel(own, c0, c1, c2, c3, out, side, pad, cols):
    step = pl.program_id(0)

    @pl.when(step == 0)
    def _():
        place = digits()
        at = place["z"] * 2
        for s, value in enumerate((c0, c1, c2, c3)):
            cols[:, eight(((place["y"] - s) & 3) * 8), :] = value[...]
        pad[...] = jnp.zeros((128, 128), F32)
        for r in range(4):
            for half in range(2):
                pad[2 * r + half : 2 * r + half + 1, :] = own[r, pl.ds(at + half, 1), :] * 0.25
        flipped = pad[...].T
        for r in range(4):
            for half in range(2):
                column = flipped[:, 2 * r + half : 2 * r + half + 1]
                side[r, 128 * half : 128 * half + 128, :] = jnp.broadcast_to(column, (128, 128))

    for group in range(4):
        rows = eight(step * 32 + group * 8)
        factors = [side[r, rows, :] for r in range(4)]
        for k in range(32):
            total = factors[0] * cols[0, k : k + 1, :]
            for r in range(1, 4):
                total = total + factors[r] * cols[r, k : k + 1, :]
            out[8 * group : 8 * group + 8, 128 * k : 128 * k + 128] = total


def call(kernel, outs, scratch, *args, flops=1 << 20, specs=None):
    size = sum(int(np.prod(s)) * 4 for s in outs)
    return pl.pallas_call(
        kernel,
        out_shape=[jax.ShapeDtypeStruct(s, F32) for s in outs],
        in_specs=specs or [VMEM] * len(args),
        out_specs=[VMEM] * len(outs),
        scratch_shapes=[pltpu.VMEM(s, F32) if isinstance(s, tuple) else s for s in scratch],
        compiler_params=PARAMS,
        cost_estimate=pl.CostEstimate(flops=flops, bytes_accessed=2 * size, transcendentals=0),
    )(*args)


def ring(axis, step):
    stride = 1 << SHIFT[axis]
    pairs = []
    for device in range(64):
        digit = device // stride % 4
        pairs.append((device, device + ((digit + step) % 4 - digit) * stride))
    return pairs


def swap_blocks(blocks, axis):
    moved = {step: lax.ppermute(blocks[step], "tm", ring(axis, step)) for step in (1, 3, 2)}
    return [blocks[0], moved[1], moved[2], moved[3]]


def swap_plane(value):
    groups = [[16 * x + 4 * y + z for x in range(4) for y in range(4)] for z in range(4)]
    return lax.all_to_all(
        value, "tm", split_axis=0, concat_axis=0, axis_index_groups=groups, tiled=True
    )


FWD = (16, 16, 1024)
INV = (16, 128, 128)


def on_device(seed_field):
    table = tables()
    tm = lax.axis_index("tm")
    ix, iy, iz = tm // 16, tm // 4 % 4, tm % 4

    seed = seed_field.reshape(2, HOPS, HOP)
    last = seed_field[0, :, LOCAL - TAPS :].reshape(8, 128)
    last = lax.ppermute(last, "tm", [(d, (d + 1) % 64) for d in range(64)]).reshape(2, TAPS)
    spots = (tm * LOCAL - TAPS + jnp.arange(TAPS, dtype=jnp.int32)) & (NT - 1)
    halo = ((last[0] + pulse_of(spots)) ** 2 + last[1] ** 2)[None, :]

    value = call(
        start_kernel, [FWD],
        [(136, 1024), (128, 1024), pltpu.VMEM((2, 768, 256), BF16), pltpu.SemaphoreType.DMA],
        seed, halo, table["toeplitz"], specs=[VMEM, VMEM, HBM],
    )[0]
    value = swap_plane(value)
    blocks = call(fwd_kernel, [(4, 16, 1024)] * 4, [(4, 4, 16, 1024)], value)
    blocks = swap_blocks(blocks, "z")
    value = call(mid_kernel, [FWD], [], *blocks)[0]
    value = swap_plane(value)
    number = (
        (iz + 4 * iy + 16 * ix)
        + 8192 * jnp.arange(4, dtype=jnp.int32)[:, None, None]
        + 64 * jnp.arange(128, dtype=jnp.int32)[None, :, None]
        + 32768 * jnp.arange(256, dtype=jnp.int32)[None, None, :]
    ).reshape(512, 256)
    freq = jnp.where(number < NT // 2, number, number - NT)
    angle = (2.0 * math.pi / (1 << 28)) * (freq * freq & ((1 << 28) - 1)).astype(F32)
    disp = jnp.stack([jnp.cos(angle), jnp.sin(angle)])
    value = call(
        spectrum_kernel, [(16, 136, 128)],
        [(256, 1024), (512, 512), (512, 512), (1024, 256), (128, 256), (256, 128), (128, 128)],
        value, table["hop_fwd"], table["cross"], table["sub_fwd"], disp, table["sub_inv"], table["hop_inv"],
    )[0]
    value = swap_plane(value)
    blocks = call(unmid_kernel, [(520, 128)] * 4, [], value)
    blocks = swap_blocks(blocks, "z")
    value, bins = call(inv_kernel, [INV, (8, 128)], [(4, 512, 128)], *blocks)
    value = swap_plane(value)

    tail = lax.ppermute(value[:, :, 0], "tm", [((d + 1) % 64, d) for d in range(64)])

    alike = [bins] + [
        lax.ppermute(bins, "grp", [(g, (g + step) % 4) for g in range(4)]) for step in (1, 2, 3)
    ]
    normal = call(normal_kernel, [(4, 8, 128)], [], *alike)[0]
    pairs = []
    for g in range(4):
        for d in range(64):
            pairs.append((g * 64 + d, d // 16 * 64 + g * 16 + d % 16))
    columns = lax.ppermute(normal, ("grp", "tm"), pairs)
    columns = [columns] + [lax.ppermute(columns, "tm", ring("y", step)) for step in (1, 2, 3)]

    correlation = pl.pallas_call(
        correlation_kernel,
        grid=(8,),
        out_shape=jax.ShapeDtypeStruct((256, 4096), F32),
        in_specs=[pl.BlockSpec((4, 8, 128), lambda i: (0, 0, 0))] * 5,
        out_specs=pl.BlockSpec((32, 4096), lambda i: (i, 0)),
        scratch_shapes=[
            pltpu.VMEM((4, 256, 128), F32), pltpu.VMEM((128, 128), F32), pltpu.VMEM((4, 32, 128), F32)
        ],
        compiler_params=PARAMS,
        cost_estimate=pl.CostEstimate(flops=1 << 23, bytes_accessed=1 << 22, transcendentals=0),
    )(normal, *columns)
    spectrogram = call(
        frames_kernel, [(HOPS, W)], [(16, 256, 128)], value, tail, table["frames"]
    )[0]
    return spectrogram[None], correlation


def solution(mesh):
    return jax.shard_map(
        on_device,
        mesh=mesh,
        in_specs=(P("grp", None, "tm"),),
        out_specs=(P("grp", "tm", None), P("tm", "grp")),
        check_vma=False,
    )
```

```python
import functools
import math

import jax
import jax.numpy as jnp
import ml_dtypes
import numpy as np
from jax import lax
from jax.experimental import pallas as pl
from jax.experimental.pallas import tpu as pltpu
from jax.sharding import PartitionSpec as P

NT = 1 << 23
LOCAL = 1 << 17
HOPS = 128
HOP = 1024
W = 2048
BINS = 16384
TAPS = 512
BIN_WIDTH = 512
PEAK_AMPLITUDE = 2.0
KERR_GAIN = 0.5
RAMAN_SHARE = 0.18
RESPONSE_FAST = 12.2
RESPONSE_SLOW = 32.0
RESPONSE_SCALE = (12.2 * 12.2 + 32.0 * 32.0) / (12.2 * 32.0 * 32.0)
FLOOR_SHARE = 0.5
F32 = jnp.float32
BF16 = jnp.bfloat16
VMEM = pl.BlockSpec(memory_space=pltpu.VMEM)
HBM = pl.BlockSpec(memory_space=pltpu.HBM)
PARAMS = pltpu.CompilerParams(vmem_limit_bytes=24 << 20)


def split_const(table):
    table = np.asarray(table, np.float64)
    high = table.astype(ml_dtypes.bfloat16)
    low = (table - high.astype(np.float64)).astype(ml_dtypes.bfloat16)
    return np.stack([high, low])


def left_form(matrix):
    return np.block([[matrix.real, -matrix.imag], [matrix.imag, matrix.real]])


def right_form(matrix):
    return np.block([[matrix.real, matrix.imag], [-matrix.imag, matrix.real]])


def dft(size, sign):
    index = np.arange(size)
    return np.exp(sign * 2j * np.pi * (index[:, None] * index[None, :] % size) / size)


def row_order():
    row = np.arange(256)
    return row // 16 + 16 * (row % 16)


@functools.lru_cache(maxsize=None)
def tables():
    out = {}
    lag = np.arange(256)[None, :] - np.arange(256)[:, None]
    taps = np.arange(TAPS)
    response = RESPONSE_SCALE * np.exp(-taps / RESPONSE_SLOW) * np.sin(taps / RESPONSE_FAST)
    blocks = []
    for step in range(3):
        position = 256 * step + lag
        inside = (position >= 0) & (position < TAPS)
        blocks.append(np.where(inside, response[np.clip(position, 0, TAPS - 1)], 0.0))
    out["toeplitz"] = split_const(np.concatenate(blocks, 0))
    rows = np.arange(256).reshape(2, 16, 8).transpose(1, 0, 2).reshape(256)
    forward = dft(256, -1)
    inverse = dft(256, 1)[row_order()] / NT
    squares = [left_form(dft(128, -1))[:, rows], right_form(dft(128, 1))]
    squares += [forward.real, forward.imag, inverse.real, inverse.imag]
    out["squares"] = np.concatenate([split_const(square) for square in squares])
    order = np.arange(256).reshape(2, 2, 64).transpose(1, 0, 2).reshape(256)
    out["frames"] = split_const(left_form(dft(128, -1))[:, order])
    return out


def halves(value):
    high = value.astype(BF16)
    low = (value - high.astype(F32)).astype(BF16)
    return high, low


def dims(contract):
    return (contract, ((), ()))


NN = ((1,), (0,))
NT_FORM = ((1,), (1,))


def dot_right(value, table, contract=NN):
    high, low = halves(value)
    dot = lambda a, b: lax.dot_general(a, b, dims(contract), preferred_element_type=F32)
    return dot(high, table[0]) + (dot(high, table[1]) + dot(low, table[0]))


def dot_left(table, value, contract=NN):
    high, low = halves(value)
    dot = lambda a, b: lax.dot_general(a, b, dims(contract), preferred_element_type=F32)
    return dot(table[0], high) + (dot(table[1], high) + dot(table[0], low))


def cmul(a, b):
    return (a[0] * b[0] - a[1] * b[1], a[0] * b[1] + a[1] * b[0])


def quad(x, sign):
    s02 = (x[0][0] + x[2][0], x[0][1] + x[2][1])
    d02 = (x[0][0] - x[2][0], x[0][1] - x[2][1])
    s13 = (x[1][0] + x[3][0], x[1][1] + x[3][1])
    d13 = (x[1][0] - x[3][0], x[1][1] - x[3][1])
    turned = (-sign * d13[1], sign * d13[0])
    return [
        (s02[0] + s13[0], s02[1] + s13[1]),
        (d02[0] + turned[0], d02[1] + turned[1]),
        (s02[0] - s13[0], s02[1] - s13[1]),
        (d02[0] - turned[0], d02[1] - turned[1]),
    ]


def powers(first):
    second = (first[0] * first[0] - first[1] * first[1], 2.0 * first[0] * first[1])
    return [None, first, second, cmul(first, second)]


def twist(values, factors):
    return [values[0]] + [cmul(values[k], factors[k]) for k in (1, 2, 3)]


def sincos(x):
    turns = jnp.floor(x * (2.0 / math.pi) + 0.5)
    rest = ((x - turns * 1.5703125) - turns * 4.837512969970703125e-4) - turns * 7.549789948768648e-8
    sq = rest * rest
    sine = rest + rest * sq * (
        -1.6666654611e-1 + sq * (8.3321608736e-3 + sq * -1.9515295891e-4)
    )
    cosine = 1.0 - 0.5 * sq + sq * sq * (
        4.166664568298827e-2 + sq * (-1.388731625493765e-3 + sq * 2.443315711809948e-5)
    )
    part = turns.astype(jnp.int32)
    odd = (part & 1) == 1
    s_val = jnp.where(odd, cosine, sine)
    c_val = jnp.where(odd, sine, cosine)
    s_val = jnp.where((part & 2) == 2, -s_val, s_val)
    c_val = jnp.where(((part + 1) & 2) == 2, -c_val, c_val)
    return s_val, c_val


def pulse_of(position):
    offset = (position - NT // 2).astype(F32) * (16.0 / NT)
    fall = jnp.exp(-jnp.abs(offset))
    return (2.0 * PEAK_AMPLITUDE) * fall / (1.0 + fall * fall)


SHIFT = {"x": 4, "y": 2, "z": 0}


def digits():
    tm = lax.axis_index("tm")
    return {axis: (tm >> SHIFT[axis]) & 3 for axis in SHIFT}


def iota(shape, axis):
    return lax.broadcasted_iota(jnp.int32, shape, axis)


def phasor(number, span, sign):
    sine, cosine = sincos((sign * 2.0 * math.pi / span) * number.astype(F32))
    return cosine, sine


def turn(number, span, sign):
    angle = sign * 2.0 * math.pi * number / span
    return math.cos(angle), math.sin(angle)


def eight(start):
    return pl.ds(pl.multiple_of(start, 8), 8)


def start_kernel(seed, halo, toep_hbm, out, buf, fre, toep, sem):
    copy = pltpu.make_async_copy(toep_hbm, toep, sem)
    copy.start()
    base = lax.axis_index("tm") * LOCAL
    buf[0:8, 512:1024] = jnp.broadcast_to(halo[...], (8, 512))

    def fill(step, carry):
        rows = eight(step * 8)
        row = iota((8, 1024), 0) + step * 8
        value = seed[0, rows, :] + pulse_of(base + row * 1024 + iota((8, 1024), 1))
        other = seed[1, rows, :]
        fre[rows, :] = value
        buf[eight(step * 8 + 8), :] = value * value + other * other
        return carry

    lax.fori_loop(0, 16, fill, 0)
    copy.wait()
    own = [halves(buf[8:136, 256 * e : 256 * e + 256]) for e in range(4)]
    back = {e: halves(buf[7:135, 256 * e : 256 * e + 256]) for e in (2, 3)}
    for e in range(4):
        total = None
        for step in range(3):
            at = e - step
            high, low = own[at] if at >= 0 else back[at + 4]
            t_high = toep[0, 256 * step : 256 * step + 256, :]
            t_low = toep[1, 256 * step : 256 * step + 256, :]
            term = (
                jnp.dot(high, t_high, preferred_element_type=F32)
                + jnp.dot(high, t_low, preferred_element_type=F32)
                + jnp.dot(low, t_high, preferred_element_type=F32)
            )
            total = term if total is None else total + term
        lanes = slice(256 * e, 256 * e + 256)
        phase = KERR_GAIN * ((1.0 - RAMAN_SHARE) * buf[8:136, lanes] + RAMAN_SHARE * total)
        sine, cosine = sincos(phase)
        value = fre[:, lanes]
        other = seed[1, :, lanes]
        out[:, 0:8, lanes] = (value * cosine - other * sine).reshape(16, 8, 256)
        out[:, 8:16, lanes] = (value * sine + other * cosine).reshape(16, 8, 256)


def sixteen(x, sign):
    inner = [quad([x[4 * a1 + a0] for a1 in range(4)], sign) for a0 in range(4)]
    out = []
    for c0 in range(4):
        row = [inner[a0][c0] for a0 in range(4)]
        row = [cmul(v, turn(a0 * c0, 16, sign)) if a0 * c0 else v for a0, v in enumerate(row)]
        out.append(quad(row, sign))
    return out


def many_powers(first):
    out = [None, first]
    for k in range(2, 16):
        out.append(cmul(out[k // 2], out[k - k // 2]))
    return out


def lanes_at(step):
    return pl.ds(pl.multiple_of(step * 128, 128), 128)


def fwd_kernel(blocks, o0, o1, o2, o3, scratch):
    place = digits()
    block = 4 * place["x"] + place["y"]
    number = place["z"] * LOCAL + (8 * block + iota((8, 128), 0)) * 1024 + iota((8, 128), 1)
    forward = turn(128, NT, -1)

    def body(step, factor):
        lanes = lanes_at(step)
        y = sixteen([(blocks[t, 0:8, lanes], blocks[t, 8:16, lanes]) for t in range(16)], -1.0)
        factors = many_powers(factor)
        for c0 in range(4):
            slot = (c0 - place["z"]) & 3
            for c1 in range(4):
                value = y[c0][c1]
                if c0 + c1:
                    value = cmul(value, factors[c0 + 4 * c1])
                scratch[slot, c1, 0:8, lanes] = value[0]
                scratch[slot, c1, 8:16, lanes] = value[1]
        for j, out in enumerate((o0, o1, o2, o3)):
            out[:, :, lanes] = scratch[j, :, :, lanes]
        return cmul(factor, forward)

    lax.fori_loop(0, 8, body, phasor(number, NT, -1))


def mid_kernel(r0, r1, r2, r3, out):
    place = digits()
    block = 4 * place["x"] + place["y"]
    number = (8 * block + iota((8, 128), 0)) * 1024 + iota((8, 128), 1) + place["z"] * LOCAL
    forward = turn(128, 4 * LOCAL, -1)

    def body(step, factor):
        lanes = lanes_at(step)
        factors = powers(factor)
        for kk in range(4):
            x = [(r[kk, 0:8, lanes], r[kk, 8:16, lanes]) for r in (r0, r1, r2, r3)]
            for ka, value in enumerate(twist(quad(x, 1.0), factors)):
                out[4 * ka + kk, 0:8, lanes] = value[0]
                out[4 * ka + kk, 8:16, lanes] = value[1]
        return cmul(factor, forward)

    lax.fori_loop(0, 8, body, phasor(number, 4 * LOCAL, -1))


def spectrum_kernel(blocks, squares, disp, out, wide, work, back, rows_w, bins, flip, flat):
    hop, unhop = squares.at[0:2], squares.at[2:4]
    fwd_c, fwd_s, inv_c, inv_s = [squares.at[2 * k : 2 * k + 2] for k in range(2, 6)]
    for part in range(4):
        lanes = slice(256 * part, 256 * part + 256)
        wide[:, lanes] = dot_left(hop, blocks[:, :, lanes].reshape(256, 256))
    lane_f = powers(phasor(iota((8, 256), 1), 1024, -1))
    number = [256 * part + iota((8, 256), 1) for part in range(4)]
    cross_first = tuple(phasor(iota((8, 256), 0) * n, LOCAL, -1) for n in number)
    cross_step = [phasor(8 * n, LOCAL, -1) for n in number]

    def body(step, carry):
        rows, low_rows = eight(step * 8), eight(step * 8 + 128)
        x = []
        for part in range(4):
            lanes = slice(256 * part, 256 * part + 256)
            x.append(cmul((wide[rows, lanes], wide[low_rows, lanes]), carry[part]))
        y = twist(quad(x, -1.0), lane_f)
        for k in range(4):
            at = eight(step * 8 + 128 * k)
            work[at, 0:256] = y[k][0]
            work[at, 256:512] = y[k][1]
        return tuple(cmul(value, move) for value, move in zip(carry, cross_step))

    lax.fori_loop(0, 16, body, cross_first)
    bins[64:128, :] = jnp.zeros((64, 256), F32)
    for k in range(4):
        rows = slice(128 * k, 128 * k + 128)
        re, im = work[rows, 0:256], work[rows, 256:512]
        re, im = (
            dot_right(re, fwd_c) - dot_right(im, fwd_s),
            dot_right(re, fwd_s) + dot_right(im, fwd_c),
        )
        power = (re * re + im * im).reshape(16, 8, 256)
        bins[16 * k : 16 * k + 16, :] = jnp.sum(power, axis=1) * (1.0 / (NT * BIN_WIDTH))
        re, im = cmul((re, im), (disp[0, rows, :], disp[1, rows, :]))
        work[rows, 0:256] = re
        work[rows, 256:512] = im
    for half in range(2):
        flip[128 * half : 128 * half + 128, :] = bins[:, 128 * half : 128 * half + 128].T
    flat[...] = flip[pl.ds(0, 128, stride=2), :] + pltpu.roll(flip[pl.ds(1, 128, stride=2), :], 64, 1)
    for dest in range(16):
        out[dest, 128:136, :] = flat[8 * dest : 8 * dest + 8, :]
    re, im = work[:, 0:256], work[:, 256:512]
    back[0:256, :] = dot_left(inv_c, re, NT_FORM) - dot_left(inv_s, im, NT_FORM)
    back[256:512, :] = dot_left(inv_c, im, NT_FORM) + dot_left(inv_s, re, NT_FORM)
    first = phasor(16 * iota((8, 128), 0), 1024, 1)
    forward, half_turn = turn(1, 1024, 1), turn(128, 1024, 1)
    freq = iota((8, 128), 1)
    cross_first = phasor(16 * iota((8, 128), 0) * freq, LOCAL, 1)
    cross_step, cross_half = phasor(freq, LOCAL, 1), phasor(128 * freq, LOCAL, 1)
    cross_part = powers(phasor(256 * freq, LOCAL, 1))

    def tail(a, carry):
        factor, other = carry
        for half in range(2):
            rows, low_rows = eight(a * 16 + 8 * half), eight(a * 16 + 8 * half + 256)
            x = [
                (back[rows, 128 * k : 128 * k + 128], back[low_rows, 128 * k : 128 * k + 128])
                for k in range(4)
            ]
            now = cmul(factor, half_turn) if half else factor
            after = cmul(other, cross_half) if half else other
            y = twist(quad(twist(x, powers(now)), 1.0), cross_part)
            for part in range(4):
                value = cmul(y[part], after)
                at = eight(a * 64 + part * 16 + 8 * half)
                rows_w[at, 0:128] = value[0]
                rows_w[at, 128:256] = value[1]
        return cmul(factor, forward), cmul(other, cross_step)

    lax.fori_loop(0, 16, tail, (first, cross_first))
    for part in range(4):
        got = dot_right(rows_w[256 * part : 256 * part + 256, :], unhop)
        for a in range(4):
            out[4 * part + a, 0:64, :] = got[64 * a : 64 * a + 64, 0:128]
            out[4 * part + a, 64:128, :] = got[64 * a : 64 * a + 64, 128:256]


def unmid_kernel(blocks, o0, o1, o2, o3):
    place = digits()
    outs = (o0, o1, o2, o3)
    total = blocks[0, 128:136, :]
    for k in range(1, 16):
        total = total + blocks[k, 128:136, :]
    for out in outs:
        out[520:528, :] = total
    block = 4 * place["x"] + place["y"]
    number = block + 16 * iota((8, 128), 0) + 1024 * iota((8, 128), 1) + place["z"] * LOCAL
    forward = turn(128, 4 * LOCAL, 1)

    def body(step, factor):
        rows, low_rows = eight(step * 8), eight(step * 8 + 64)
        factors = powers(factor)
        for kk in range(4):
            x = [(blocks[4 * ka + kk, rows, :], blocks[4 * ka + kk, low_rows, :]) for ka in range(4)]
            for out, value in zip(outs, quad(twist(x, factors), 1.0)):
                out[eight(step * 8 + 128 * kk), :] = value[0]
                out[eight(step * 8 + 128 * kk + 64), :] = value[1]
        return cmul(factor, forward)

    lax.fori_loop(0, 8, body, phasor(number, 4 * LOCAL, 1))
    pick = jnp.where(iota((16, 128), 1) == 0, 1.0, 0.0).astype(BF16)
    for j in range(4):
        high, low = halves(outs[(j + 1) % 4][0:512, :])
        row = lax.dot_general(pick, high, dims(NT_FORM), preferred_element_type=F32)
        row = row + lax.dot_general(pick, low, dims(NT_FORM), preferred_element_type=F32)
        for kk in range(4):
            outs[j][512 + kk : 513 + kk, :] = row[0:1, 128 * kk : 128 * kk + 128]
        outs[j][516:520, :] = jnp.zeros((4, 128), F32)


def unsixteen(x, factors):
    line = [None] * 16
    for c0 in range(4):
        for c1 in range(4):
            value = x[c0][c1]
            line[4 * c1 + c0] = cmul(value, factors[c0 + 4 * c1]) if c0 + c1 else value
    return sixteen(line, 1.0)


def inv_kernel(r0, r1, r2, r3, out, bins, blocks):
    place = digits()
    bins[...] = (r0[520:528, :] + r1[520:528, :]) + (r2[520:528, :] + r3[520:528, :])
    for s, value in enumerate((r0, r1, r2, r3)):
        blocks[(place["z"] - s) & 3] = value[0:520, :]
    block = 4 * place["x"] + place["y"]
    number = place["z"] * LOCAL + block + 16 * iota((8, 128), 0) + 1024 * iota((8, 128), 1)
    forward = turn(128, NT, 1)

    def body(step, factor):
        x = [
            [
                (blocks[c0, eight(step * 8 + 128 * c1), :], blocks[c0, eight(step * 8 + 128 * c1 + 64), :])
                for c1 in range(4)
            ]
            for c0 in range(4)
        ]
        y = unsixteen(x, many_powers(factor))
        for a0 in range(4):
            for a1 in range(4):
                out[4 * a1 + a0, eight(step * 8), :] = y[a0][a1][0]
                out[4 * a1 + a0, eight(step * 8 + 64), :] = y[a0][a1][1]
        return cmul(factor, forward)

    lax.fori_loop(0, 8, body, phasor(number, NT, 1))
    after = (place["z"] + 1) & 3
    lane = iota((8, 128), 1)
    factors = many_powers(phasor(after * LOCAL + block + 16 * (lane & 63), NT, 1))
    x = []
    for c0 in range(4):
        rows = [
            jnp.broadcast_to(blocks[c0, 512 + c1 : 513 + c1, :], (8, 128)) for c1 in range(4)
        ]
        x.append([(row, pltpu.roll(row, 64, 1)) for row in rows])
    y = unsixteen(x, factors)
    flat = []
    for t in range(16):
        re, im = y[t % 4][t // 4]
        flat.append(jnp.where(lane < 64, re, pltpu.roll(im, 64, 1)))
    wrap = after == 0
    for t in range(16):
        out[t, 128:136, :] = jnp.where(wrap, flat[(t + 1) % 16], flat[t])


def frames_kernel(blocks, mat, out, got):
    columns = jnp.concatenate([blocks[a, 128:129, :] for a in range(16)], axis=0).T
    lane = iota((128, 128), 1)
    wave = phasor(16 * iota((64, 128), 0), W, 1)
    for a in range(16):
        here = blocks[a, 0:128, :]
        after = jnp.where(lane == 127, columns[:, a : a + 1], pltpu.roll(here, 127, 1))
        late = 0.5 + 0.5 * wave[0]
        early = 0.5 - 0.5 * wave[0]
        pieces = [here[0:64] * early, here[64:128] * early, after[0:64] * late, after[64:128] * late]
        got[a] = dot_left(mat, jnp.concatenate(pieces, axis=0))
        wave = cmul(wave, turn(1, W, 1))
    first = phasor(iota((8, 128), 0), W, -1)
    forward = turn(8, W, -1)

    def body(step, factor):
        rows, low_rows = eight(step * 8), eight(step * 8 + 128)
        factors = many_powers(factor)
        x = [(got[a, rows, :], got[a, low_rows, :]) for a in range(16)]
        y = sixteen([cmul(x[a], factors[a]) if a else x[a] for a in range(16)], -1.0)
        for c0 in range(4):
            for c1 in range(4):
                value = y[c0][c1]
                got[c0 + 4 * c1, rows, :] = (value[0] * value[0] + value[1] * value[1]) * (1.0 / W)
        return cmul(factor, forward)

    lax.fori_loop(0, 16, body, first)
    for c in range(16):
        out[:, 128 * c : 128 * c + 128] = got[c, 0:128, :].T


def normal_kernel(b0, b1, b2, b3, out):
    blocks = [b[...] for b in (b0, b1, b2, b3)]
    total = (blocks[0] + blocks[1]) + (blocks[2] + blocks[3])
    average = total * 0.25
    centred = [b - average for b in blocks]
    sq = [c * c for c in centred]
    variance = ((sq[0] + sq[1]) + (sq[2] + sq[3])) * 0.25
    spread = jnp.sqrt(jnp.maximum(variance, FLOOR_SHARE * average * average / BIN_WIDTH))
    grp = lax.axis_index("grp")
    for step in range(4):
        out[(grp - step) & 3] = centred[step] / spread


def correlation_kernel(own, c0, c1, c2, c3, out, side, pad, cols):
    step = pl.program_id(0)

    @pl.when(step == 0)
    def _():
        place = digits()
        at = place["z"] * 2
        for s, value in enumerate((c0, c1, c2, c3)):
            cols[:, eight(((place["y"] - s) & 3) * 8), :] = value[...]
        pad[...] = jnp.zeros((128, 128), F32)
        for r in range(4):
            for half in range(2):
                pad[2 * r + half : 2 * r + half + 1, :] = own[r, pl.ds(at + half, 1), :] * 0.25
        flipped = pad[...].T
        for r in range(4):
            for half in range(2):
                column = flipped[:, 2 * r + half : 2 * r + half + 1]
                side[r, 128 * half : 128 * half + 128, :] = jnp.broadcast_to(column, (128, 128))

    for half in range(2):
        base = 32 * half
        factors = [[side[r, eight(step * 64 + base + g * 8), :] for r in range(4)] for g in range(4)]
        for k in range(32):
            line = [jnp.broadcast_to(cols[r, k : k + 1, :], (8, 128)) for r in range(4)]
            for g in range(4):
                total = (factors[g][0] * line[0] + factors[g][1] * line[1]) + (
                    factors[g][2] * line[2] + factors[g][3] * line[3]
                )
                at = base + 8 * g
                out[at : at + 8, 128 * k : 128 * k + 128] = total


def call(kernel, outs, scratch, *args, flops=1 << 20, specs=None):
    size = sum(int(np.prod(s)) * 4 for s in outs)
    return pl.pallas_call(
        kernel,
        out_shape=[jax.ShapeDtypeStruct(s, F32) for s in outs],
        in_specs=specs or [VMEM] * len(args),
        out_specs=[VMEM] * len(outs),
        scratch_shapes=[pltpu.VMEM(s, F32) if isinstance(s, tuple) else s for s in scratch],
        compiler_params=PARAMS,
        cost_estimate=pl.CostEstimate(flops=flops, bytes_accessed=2 * size, transcendentals=0),
    )(*args)


def ring(axis, step):
    stride = 1 << SHIFT[axis]
    pairs = []
    for device in range(64):
        digit = device // stride % 4
        pairs.append((device, device + ((digit + step) % 4 - digit) * stride))
    return pairs


def swap_z(blocks):
    moved = {step: lax.ppermute(blocks[step], "tm", ring("z", step)) for step in (2, 1, 3)}
    return [blocks[0], moved[1], moved[2], moved[3]]


def swap_plane(value):
    groups = [[16 * x + 4 * y + z for x in range(4) for y in range(4)] for z in range(4)]
    return lax.all_to_all(
        value, "tm", split_axis=0, concat_axis=0, axis_index_groups=groups, tiled=True
    )


FWD = (16, 16, 1024)


def on_device(seed_field):
    table = tables()
    tm = lax.axis_index("tm")
    ix, iy, iz = tm // 16, tm // 4 % 4, tm % 4

    seed = seed_field.reshape(2, HOPS, HOP)
    last = seed_field[0, :, LOCAL - TAPS :].reshape(8, 128)
    last = lax.ppermute(last, "tm", [(d, (d + 1) % 64) for d in range(64)]).reshape(2, TAPS)
    spots = (tm * LOCAL - TAPS + jnp.arange(TAPS, dtype=jnp.int32)) & (NT - 1)
    halo = ((last[0] + pulse_of(spots)) ** 2 + last[1] ** 2)[None, :]

    value = call(
        start_kernel, [FWD],
        [(136, 1024), (128, 1024), pltpu.VMEM((2, 768, 256), BF16), pltpu.SemaphoreType.DMA],
        seed, halo, table["toeplitz"], specs=[VMEM, VMEM, HBM],
    )[0]
    value = swap_plane(value)
    blocks = call(fwd_kernel, [(4, 16, 1024)] * 4, [(4, 4, 16, 1024)], value)
    blocks = swap_z(blocks)
    value = call(mid_kernel, [FWD], [], *blocks)[0]
    value = swap_plane(value)
    number = (
        (iz + 4 * iy + 16 * ix)
        + 8192 * jnp.arange(4, dtype=jnp.int32)[:, None, None]
        + 64 * jnp.arange(128, dtype=jnp.int32)[None, :, None]
        + 32768 * jnp.arange(256, dtype=jnp.int32)[None, None, :]
    ).reshape(512, 256)
    freq = jnp.where(number < NT // 2, number, number - NT)
    angle = (2.0 * math.pi / (1 << 28)) * (freq * freq & ((1 << 28) - 1)).astype(F32)
    disp = jnp.stack([jnp.cos(angle), jnp.sin(angle)])
    value = call(
        spectrum_kernel, [(16, 136, 128)],
        [(256, 1024), (512, 512), (512, 512), (1024, 256), (128, 256), (256, 128), (128, 128)],
        value, table["squares"], disp,
    )[0]
    value = swap_plane(value)
    blocks = call(unmid_kernel, [(528, 128)] * 4, [], value)
    blocks = swap_z(blocks)
    value, bins = call(inv_kernel, [(16, 136, 128), (8, 128)], [(4, 520, 128)], *blocks)
    value = swap_plane(value)

    alike = [bins] + [
        lax.ppermute(bins, "grp", [(g, (g + step) % 4) for g in range(4)]) for step in (1, 2, 3)
    ]
    normal = call(normal_kernel, [(4, 8, 128)], [], *alike)[0]
    columns = []
    for step in range(4):
        pairs = []
        for g in range(4):
            for d in range(64):
                x, y, z = d // 16, d // 4 % 4, d % 4
                pairs.append((g * 64 + d, x * 64 + g * 16 + (y + step) % 4 * 4 + z))
        columns.append(lax.ppermute(normal, ("grp", "tm"), pairs))

    spectrogram = call(frames_kernel, [(HOPS, W)], [(16, 256, 128)], value, table["frames"])[0]
    spectrogram, normal, *columns = lax.optimization_barrier((spectrogram, normal, *columns))
    correlation = pl.pallas_call(
        correlation_kernel,
        grid=(4,),
        out_shape=jax.ShapeDtypeStruct((256, 4096), F32),
        in_specs=[pl.BlockSpec((4, 8, 128), lambda i: (0, 0, 0))] * 5,
        out_specs=pl.BlockSpec((64, 4096), lambda i: (i, 0)),
        scratch_shapes=[
            pltpu.VMEM((4, 256, 128), F32), pltpu.VMEM((128, 128), F32), pltpu.VMEM((4, 32, 128), F32)
        ],
        compiler_params=PARAMS,
        cost_estimate=pl.CostEstimate(flops=1 << 23, bytes_accessed=1 << 22, transcendentals=0),
    )(normal, *columns)
    return spectrogram[None], correlation


def solution(mesh):
    return jax.shard_map(
        on_device,
        mesh=mesh,
        in_specs=(P("grp", None, "tm"),),
        out_specs=(P("grp", "tm", None), P("tm", "grp")),
        check_vma=False,
    )
```

```python
import functools
import math

import jax
import jax.numpy as jnp
import ml_dtypes
import numpy as np
from jax import lax
from jax.experimental import pallas as pl
from jax.experimental.pallas import tpu as pltpu
from jax.sharding import PartitionSpec as P

NT = 1 << 23
LOCAL = 1 << 17
HOPS = 128
HOP = 1024
W = 2048
BINS = 16384
TAPS = 512
BIN_WIDTH = 512
PEAK_AMPLITUDE = 2.0
KERR_GAIN = 0.5
RAMAN_SHARE = 0.18
RESPONSE_FAST = 12.2
RESPONSE_SLOW = 32.0
RESPONSE_SCALE = (12.2 * 12.2 + 32.0 * 32.0) / (12.2 * 32.0 * 32.0)
FLOOR_SHARE = 0.5
F32 = jnp.float32
BF16 = jnp.bfloat16
VMEM = pl.BlockSpec(memory_space=pltpu.VMEM)
HBM = pl.BlockSpec(memory_space=pltpu.HBM)
PARAMS = pltpu.CompilerParams(vmem_limit_bytes=24 << 20)


def split_const(table):
    table = np.asarray(table, np.float64)
    high = table.astype(ml_dtypes.bfloat16)
    low = (table - high.astype(np.float64)).astype(ml_dtypes.bfloat16)
    return np.stack([high, low])


def left_form(matrix):
    return np.block([[matrix.real, -matrix.imag], [matrix.imag, matrix.real]])


def right_form(matrix):
    return np.block([[matrix.real, matrix.imag], [-matrix.imag, matrix.real]])


def dft(size, sign):
    index = np.arange(size)
    return np.exp(sign * 2j * np.pi * (index[:, None] * index[None, :] % size) / size)


def row_order():
    row = np.arange(256)
    return row // 16 + 16 * (row % 16)


@functools.lru_cache(maxsize=None)
def tables():
    out = {}
    lag = np.arange(256)[None, :] - np.arange(256)[:, None]
    taps = np.arange(TAPS)
    response = RESPONSE_SCALE * np.exp(-taps / RESPONSE_SLOW) * np.sin(taps / RESPONSE_FAST)
    blocks = []
    for step in range(3):
        position = 256 * step + lag
        inside = (position >= 0) & (position < TAPS)
        blocks.append(np.where(inside, response[np.clip(position, 0, TAPS - 1)], 0.0))
    out["toeplitz"] = split_const(np.concatenate(blocks, 0))
    rows = np.arange(256).reshape(2, 16, 8).transpose(1, 0, 2).reshape(256)
    forward = dft(256, -1)
    inverse = dft(256, 1)[row_order()] / NT
    squares = [left_form(dft(128, -1))[:, rows], right_form(dft(128, 1))]
    squares += [forward.real, forward.imag, inverse.real, inverse.imag]
    out["squares"] = np.concatenate([split_const(square) for square in squares])
    order = np.arange(256).reshape(2, 2, 64).transpose(1, 0, 2).reshape(256)
    out["frames"] = split_const(left_form(dft(128, -1))[:, order])
    return out


def halves(value):
    high = value.astype(BF16)
    low = (value - high.astype(F32)).astype(BF16)
    return high, low


def dims(contract):
    return (contract, ((), ()))


NN = ((1,), (0,))
NT_FORM = ((1,), (1,))


def dot_right(values, tables):
    left, right = [], []
    for value, table in zip(values, tables):
        high, low = halves(value)
        left += [low, high, high]
        right += [table[0], table[1], table[0]]
    left, right = jnp.concatenate(left, axis=1), jnp.concatenate(right, axis=0)
    return jnp.dot(left, right, preferred_element_type=F32)


def dot_left(tables, values, contract=NN):
    left, right = [], []
    for value, table in zip(values, tables):
        high, low = halves(value)
        left += [table[0], table[1], table[0]]
        right += [low, high, high]
    left, right = jnp.concatenate(left, axis=1), jnp.concatenate(right, axis=contract[1][0])
    return lax.dot_general(left, right, dims(contract), preferred_element_type=F32)


def cmul(a, b):
    return (a[0] * b[0] - a[1] * b[1], a[0] * b[1] + a[1] * b[0])


def quad(x, sign):
    s02 = (x[0][0] + x[2][0], x[0][1] + x[2][1])
    d02 = (x[0][0] - x[2][0], x[0][1] - x[2][1])
    s13 = (x[1][0] + x[3][0], x[1][1] + x[3][1])
    d13 = (x[1][0] - x[3][0], x[1][1] - x[3][1])
    turned = (-sign * d13[1], sign * d13[0])
    return [
        (s02[0] + s13[0], s02[1] + s13[1]),
        (d02[0] + turned[0], d02[1] + turned[1]),
        (s02[0] - s13[0], s02[1] - s13[1]),
        (d02[0] - turned[0], d02[1] - turned[1]),
    ]


def powers(first):
    second = (first[0] * first[0] - first[1] * first[1], 2.0 * first[0] * first[1])
    return [None, first, second, cmul(first, second)]


def twist(values, factors):
    return [values[0]] + [cmul(values[k], factors[k]) for k in (1, 2, 3)]


def sincos(x):
    turns = jnp.floor(x * (2.0 / math.pi) + 0.5)
    rest = ((x - turns * 1.5703125) - turns * 4.837512969970703125e-4) - turns * 7.549789948768648e-8
    sq = rest * rest
    sine = rest + rest * sq * (
        -1.6666654611e-1 + sq * (8.3321608736e-3 + sq * -1.9515295891e-4)
    )
    cosine = 1.0 - 0.5 * sq + sq * sq * (
        4.166664568298827e-2 + sq * (-1.388731625493765e-3 + sq * 2.443315711809948e-5)
    )
    part = turns.astype(jnp.int32)
    odd = (part & 1) == 1
    s_val = jnp.where(odd, cosine, sine)
    c_val = jnp.where(odd, sine, cosine)
    s_val = jnp.where((part & 2) == 2, -s_val, s_val)
    c_val = jnp.where(((part + 1) & 2) == 2, -c_val, c_val)
    return s_val, c_val


def pulse_of(position):
    offset = (position - NT // 2).astype(F32) * (16.0 / NT)
    fall = jnp.exp(-jnp.abs(offset))
    return (2.0 * PEAK_AMPLITUDE) * fall / (1.0 + fall * fall)


SHIFT = {"x": 4, "y": 2, "z": 0}


def digits():
    tm = lax.axis_index("tm")
    return {axis: (tm >> SHIFT[axis]) & 3 for axis in SHIFT}


def iota(shape, axis):
    return lax.broadcasted_iota(jnp.int32, shape, axis)


def phasor(number, span, sign):
    sine, cosine = sincos((sign * 2.0 * math.pi / span) * number.astype(F32))
    return cosine, sine


def turn(number, span, sign):
    angle = sign * 2.0 * math.pi * number / span
    return math.cos(angle), math.sin(angle)


def eight(start):
    return pl.ds(pl.multiple_of(start, 8), 8)


def start_kernel(seed, halo, toep_hbm, out, buf, fre, toep, sem):
    copy = pltpu.make_async_copy(toep_hbm, toep, sem)
    copy.start()
    base = lax.axis_index("tm") * LOCAL
    buf[0:8, 512:1024] = jnp.broadcast_to(halo[...], (8, 512))

    def fill(step, carry):
        rows = eight(step * 8)
        row = iota((8, 1024), 0) + step * 8
        value = seed[0, rows, :] + pulse_of(base + row * 1024 + iota((8, 1024), 1))
        other = seed[1, rows, :]
        fre[rows, :] = value
        buf[eight(step * 8 + 8), :] = value * value + other * other
        return carry

    lax.fori_loop(0, 16, fill, 0, unroll=4)
    copy.wait()
    own = [halves(buf[8:136, 256 * e : 256 * e + 256]) for e in range(4)]
    back = {e: halves(buf[7:135, 256 * e : 256 * e + 256]) for e in (2, 3)}
    for e in range(4):
        left, right = [], []
        for step in range(3):
            at = e - step
            high, low = own[at] if at >= 0 else back[at + 4]
            rows = slice(256 * step, 256 * step + 256)
            left += [low, high, high]
            right += [toep[0, rows, :], toep[1, rows, :], toep[0, rows, :]]
        left, right = jnp.concatenate(left, axis=1), jnp.concatenate(right, axis=0)
        total = jnp.dot(left, right, preferred_element_type=F32)
        lanes = slice(256 * e, 256 * e + 256)
        phase = KERR_GAIN * ((1.0 - RAMAN_SHARE) * buf[8:136, lanes] + RAMAN_SHARE * total)
        sine, cosine = sincos(phase)
        value = fre[:, lanes]
        other = seed[1, :, lanes]
        out[:, 0:8, lanes] = (value * cosine - other * sine).reshape(16, 8, 256)
        out[:, 8:16, lanes] = (value * sine + other * cosine).reshape(16, 8, 256)


def sixteen(x, sign):
    inner = [quad([x[4 * a1 + a0] for a1 in range(4)], sign) for a0 in range(4)]
    out = []
    for c0 in range(4):
        row = [inner[a0][c0] for a0 in range(4)]
        row = [cmul(v, turn(a0 * c0, 16, sign)) if a0 * c0 else v for a0, v in enumerate(row)]
        out.append(quad(row, sign))
    return out


def many_powers(first):
    out = [None, first]
    for k in range(2, 16):
        out.append(cmul(out[k // 2], out[k - k // 2]))
    return out


def lanes_at(step):
    return pl.ds(pl.multiple_of(step * 128, 128), 128)


def fwd_kernel(blocks, o0, o1, o2, o3, scratch):
    place = digits()
    block = 4 * place["x"] + place["y"]
    number = place["z"] * LOCAL + (8 * block + iota((8, 128), 0)) * 1024 + iota((8, 128), 1)
    forward = turn(128, NT, -1)

    def body(step, factor):
        lanes = lanes_at(step)
        y = sixteen([(blocks[t, 0:8, lanes], blocks[t, 8:16, lanes]) for t in range(16)], -1.0)
        factors = many_powers(factor)
        for c0 in range(4):
            slot = (c0 - place["z"]) & 3
            for c1 in range(4):
                value = y[c0][c1]
                if c0 + c1:
                    value = cmul(value, factors[c0 + 4 * c1])
                scratch[slot, c1, 0:8, lanes] = value[0]
                scratch[slot, c1, 8:16, lanes] = value[1]
        for j, out in enumerate((o0, o1, o2, o3)):
            out[:, :, lanes] = scratch[j, :, :, lanes]
        return cmul(factor, forward)

    lax.fori_loop(0, 8, body, phasor(number, NT, -1), unroll=4)


def mid_kernel(r0, r1, r2, r3, out):
    place = digits()
    block = 4 * place["x"] + place["y"]
    number = (8 * block + iota((8, 128), 0)) * 1024 + iota((8, 128), 1) + place["z"] * LOCAL
    forward = turn(128, 4 * LOCAL, -1)

    def body(step, factor):
        lanes = lanes_at(step)
        factors = powers(factor)
        for kk in range(4):
            x = [(r[kk, 0:8, lanes], r[kk, 8:16, lanes]) for r in (r0, r1, r2, r3)]
            for ka, value in enumerate(twist(quad(x, 1.0), factors)):
                out[4 * ka + kk, 0:8, lanes] = value[0]
                out[4 * ka + kk, 8:16, lanes] = value[1]
        return cmul(factor, forward)

    lax.fori_loop(0, 8, body, phasor(number, 4 * LOCAL, -1), unroll=4)


def spectrum_kernel(blocks, squares, disp, out, wide, work, back, rows_w, bins, flip, flat):
    hop, unhop = squares.at[0:2], squares.at[2:4]
    fwd_c, fwd_s, inv_c, inv_s = [squares.at[2 * k : 2 * k + 2] for k in range(2, 6)]
    for part in range(4):
        lanes = slice(256 * part, 256 * part + 256)
        wide[:, lanes] = dot_left([hop], [blocks[:, :, lanes].reshape(256, 256)])
    lane_f = powers(phasor(iota((8, 256), 1), 1024, -1))
    number = [256 * part + iota((8, 256), 1) for part in range(4)]
    cross_first = tuple(phasor(iota((8, 256), 0) * n, LOCAL, -1) for n in number)
    cross_step = [phasor(8 * n, LOCAL, -1) for n in number]

    def body(step, carry):
        rows, low_rows = eight(step * 8), eight(step * 8 + 128)
        x = []
        for part in range(4):
            lanes = slice(256 * part, 256 * part + 256)
            x.append(cmul((wide[rows, lanes], wide[low_rows, lanes]), carry[part]))
        y = twist(quad(x, -1.0), lane_f)
        for k in range(4):
            at = eight(step * 8 + 128 * k)
            work[at, 0:256] = y[k][0]
            work[at, 256:512] = y[k][1]
        return tuple(cmul(value, move) for value, move in zip(carry, cross_step))

    lax.fori_loop(0, 16, body, cross_first, unroll=4)
    bins[64:128, :] = jnp.zeros((64, 256), F32)
    for k in range(4):
        rows = slice(128 * k, 128 * k + 128)
        re, im = work[rows, 0:256], work[rows, 256:512]
        re, im = dot_right([re, -im], [fwd_c, fwd_s]), dot_right([re, im], [fwd_s, fwd_c])
        power = (re * re + im * im).reshape(16, 8, 256)
        bins[16 * k : 16 * k + 16, :] = jnp.sum(power, axis=1) * (1.0 / (NT * BIN_WIDTH))
        re, im = cmul((re, im), (disp[0, rows, :], disp[1, rows, :]))
        work[rows, 0:256] = re
        work[rows, 256:512] = im
    for half in range(2):
        flip[128 * half : 128 * half + 128, :] = bins[:, 128 * half : 128 * half + 128].T
    flat[...] = flip[pl.ds(0, 128, stride=2), :] + pltpu.roll(flip[pl.ds(1, 128, stride=2), :], 64, 1)
    for dest in range(16):
        out[dest, 128:136, :] = flat[8 * dest : 8 * dest + 8, :]
    re, im = work[:, 0:256], work[:, 256:512]
    back[0:256, :] = dot_left([inv_c, inv_s], [re, -im], NT_FORM)
    back[256:512, :] = dot_left([inv_s, inv_c], [re, im], NT_FORM)
    first = phasor(16 * iota((8, 128), 0), 1024, 1)
    forward, half_turn = turn(1, 1024, 1), turn(128, 1024, 1)
    freq = iota((8, 128), 1)
    cross_first = phasor(16 * iota((8, 128), 0) * freq, LOCAL, 1)
    cross_step, cross_half = phasor(freq, LOCAL, 1), phasor(128 * freq, LOCAL, 1)
    cross_part = powers(phasor(256 * freq, LOCAL, 1))

    def tail(a, carry):
        factor, other = carry
        for half in range(2):
            rows, low_rows = eight(a * 16 + 8 * half), eight(a * 16 + 8 * half + 256)
            x = [
                (back[rows, 128 * k : 128 * k + 128], back[low_rows, 128 * k : 128 * k + 128])
                for k in range(4)
            ]
            now = cmul(factor, half_turn) if half else factor
            after = cmul(other, cross_half) if half else other
            y = twist(quad(twist(x, powers(now)), 1.0), cross_part)
            for part in range(4):
                value = cmul(y[part], after)
                at = eight(a * 64 + part * 16 + 8 * half)
                rows_w[at, 0:128] = value[0]
                rows_w[at, 128:256] = value[1]
        return cmul(factor, forward), cmul(other, cross_step)

    lax.fori_loop(0, 16, tail, (first, cross_first), unroll=4)
    for part in range(4):
        got = dot_right([rows_w[256 * part : 256 * part + 256, :]], [unhop])
        for a in range(4):
            out[4 * part + a, 0:64, :] = got[64 * a : 64 * a + 64, 0:128]
            out[4 * part + a, 64:128, :] = got[64 * a : 64 * a + 64, 128:256]


def unmid_kernel(blocks, o0, o1, o2, o3):
    place = digits()
    outs = (o0, o1, o2, o3)
    total = blocks[0, 128:136, :]
    for k in range(1, 16):
        total = total + blocks[k, 128:136, :]
    for out in outs:
        out[520:528, :] = total
    block = 4 * place["x"] + place["y"]
    number = block + 16 * iota((8, 128), 0) + 1024 * iota((8, 128), 1) + place["z"] * LOCAL
    forward = turn(128, 4 * LOCAL, 1)

    def body(step, factor):
        rows, low_rows = eight(step * 8), eight(step * 8 + 64)
        factors = powers(factor)
        for kk in range(4):
            x = [(blocks[4 * ka + kk, rows, :], blocks[4 * ka + kk, low_rows, :]) for ka in range(4)]
            for out, value in zip(outs, quad(twist(x, factors), 1.0)):
                out[eight(step * 8 + 128 * kk), :] = value[0]
                out[eight(step * 8 + 128 * kk + 64), :] = value[1]
        return cmul(factor, forward)

    lax.fori_loop(0, 8, body, phasor(number, 4 * LOCAL, 1), unroll=4)
    pick = jnp.where(iota((16, 128), 1) == 0, 1.0, 0.0).astype(BF16)
    for j in range(4):
        high, low = halves(outs[(j + 1) % 4][0:512, :])
        row = lax.dot_general(pick, high, dims(NT_FORM), preferred_element_type=F32)
        row = row + lax.dot_general(pick, low, dims(NT_FORM), preferred_element_type=F32)
        for kk in range(4):
            outs[j][512 + kk : 513 + kk, :] = row[0:1, 128 * kk : 128 * kk + 128]
        outs[j][516:520, :] = jnp.zeros((4, 128), F32)


def unsixteen(x, factors):
    line = [None] * 16
    for c0 in range(4):
        for c1 in range(4):
            value = x[c0][c1]
            line[4 * c1 + c0] = cmul(value, factors[c0 + 4 * c1]) if c0 + c1 else value
    return sixteen(line, 1.0)


def inv_kernel(r0, r1, r2, r3, out, bins, blocks):
    place = digits()
    bins[...] = (r0[520:528, :] + r1[520:528, :]) + (r2[520:528, :] + r3[520:528, :])
    for s, value in enumerate((r0, r1, r2, r3)):
        blocks[(place["z"] - s) & 3] = value[0:520, :]
    block = 4 * place["x"] + place["y"]
    number = place["z"] * LOCAL + block + 16 * iota((8, 128), 0) + 1024 * iota((8, 128), 1)
    forward = turn(128, NT, 1)

    def body(step, factor):
        x = [
            [
                (blocks[c0, eight(step * 8 + 128 * c1), :], blocks[c0, eight(step * 8 + 128 * c1 + 64), :])
                for c1 in range(4)
            ]
            for c0 in range(4)
        ]
        y = unsixteen(x, many_powers(factor))
        for a0 in range(4):
            for a1 in range(4):
                out[4 * a1 + a0, eight(step * 8), :] = y[a0][a1][0]
                out[4 * a1 + a0, eight(step * 8 + 64), :] = y[a0][a1][1]
        return cmul(factor, forward)

    lax.fori_loop(0, 8, body, phasor(number, NT, 1), unroll=4)
    after = (place["z"] + 1) & 3
    lane = iota((8, 128), 1)
    factors = many_powers(phasor(after * LOCAL + block + 16 * (lane & 63), NT, 1))
    x = []
    for c0 in range(4):
        rows = [
            jnp.broadcast_to(blocks[c0, 512 + c1 : 513 + c1, :], (8, 128)) for c1 in range(4)
        ]
        x.append([(row, pltpu.roll(row, 64, 1)) for row in rows])
    y = unsixteen(x, factors)
    flat = []
    for t in range(16):
        re, im = y[t % 4][t // 4]
        flat.append(jnp.where(lane < 64, re, pltpu.roll(im, 64, 1)))
    wrap = after == 0
    for t in range(16):
        out[t, 128:136, :] = jnp.where(wrap, flat[(t + 1) % 16], flat[t])


def frames_kernel(blocks, mat, out_hbm, got, out, sems):
    columns = jnp.concatenate([blocks[a, 128:129, :] for a in range(16)], axis=0).T
    lane = iota((128, 128), 1)
    wave = phasor(16 * iota((64, 128), 0), W, 1)
    for a in range(16):
        here = blocks[a, 0:128, :]
        after = jnp.where(lane == 127, columns[:, a : a + 1], pltpu.roll(here, 127, 1))
        late = 0.5 + 0.5 * wave[0]
        early = 0.5 - 0.5 * wave[0]
        pieces = [here[0:64] * early, here[64:128] * early, after[0:64] * late, after[64:128] * late]
        got[a] = dot_left([mat], [jnp.concatenate(pieces, axis=0)])
        wave = cmul(wave, turn(1, W, 1))
    first = phasor(iota((8, 128), 0), W, -1)
    forward = turn(8, W, -1)

    def body(step, factor):
        rows, low_rows = eight(step * 8), eight(step * 8 + 128)
        factors = many_powers(factor)
        x = [(got[a, rows, :], got[a, low_rows, :]) for a in range(16)]
        y = sixteen([cmul(x[a], factors[a]) if a else x[a] for a in range(16)], -1.0)
        for c0 in range(4):
            for c1 in range(4):
                value = y[c0][c1]
                got[c0 + 4 * c1, rows, :] = (value[0] * value[0] + value[1] * value[1]) * (1.0 / W)
        return cmul(factor, forward)

    lax.fori_loop(0, 16, body, first, unroll=4)
    copies = []
    for c in range(16):
        out[:, 128 * c : 128 * c + 128] = got[c, 0:128, :].T
        if c % 4 == 3:
            lanes = pl.ds(128 * (c - 3), 512)
            copies.append(pltpu.make_async_copy(out.at[:, lanes], out_hbm.at[:, lanes], sems.at[c // 4]))
            copies[-1].start()
    for copy in copies:
        copy.wait()


def normal_kernel(b0, b1, b2, b3, out, side, pad):
    blocks = [b[...] for b in (b0, b1, b2, b3)]
    total = (blocks[0] + blocks[1]) + (blocks[2] + blocks[3])
    average = total * 0.25
    centred = [b - average for b in blocks]
    sq = [c * c for c in centred]
    variance = ((sq[0] + sq[1]) + (sq[2] + sq[3])) * 0.25
    spread = jnp.sqrt(jnp.maximum(variance, FLOOR_SHARE * average * average / BIN_WIDTH))
    grp = lax.axis_index("grp")
    for step in range(4):
        out[(grp - step) & 3] = centred[step] / spread
    at = digits()["z"] * 2
    pad[...] = jnp.zeros((128, 128), F32)
    for r in range(4):
        for half in range(2):
            pad[2 * r + half : 2 * r + half + 1, :] = out[r, pl.ds(at + half, 1), :] * 0.25
    flipped = pad[...].T
    for r in range(4):
        for half in range(2):
            column = flipped[:, 2 * r + half : 2 * r + half + 1]
            side[r, 128 * half : 128 * half + 128, :] = jnp.broadcast_to(column, (128, 128))


def correlation_kernel(side, c0, c1, c2, c3, out, cols):
    step = pl.program_id(0)

    @pl.when(step == 0)
    def _():
        place = digits()
        for s, value in enumerate((c0, c1, c2, c3)):
            cols[:, eight(((place["y"] - s) & 3) * 8), :] = value[...]

    for half in range(2):
        base = 32 * half
        factors = [[side[r, eight(step * 64 + base + g * 8), :] for r in range(4)] for g in range(4)]
        for k in range(32):
            line = [jnp.broadcast_to(cols[r, k : k + 1, :], (8, 128)) for r in range(4)]
            for g in range(4):
                total = (factors[g][0] * line[0] + factors[g][1] * line[1]) + (
                    factors[g][2] * line[2] + factors[g][3] * line[3]
                )
                at = base + 8 * g
                out[at : at + 8, 128 * k : 128 * k + 128] = total


def call(kernel, outs, scratch, *args, flops=1 << 20, specs=None, place=VMEM):
    size = sum(int(np.prod(s)) * 4 for s in outs)
    return pl.pallas_call(
        kernel,
        out_shape=[jax.ShapeDtypeStruct(s, F32) for s in outs],
        in_specs=specs or [VMEM] * len(args),
        out_specs=[place] * len(outs),
        scratch_shapes=[pltpu.VMEM(s, F32) if isinstance(s, tuple) else s for s in scratch],
        compiler_params=PARAMS,
        cost_estimate=pl.CostEstimate(flops=flops, bytes_accessed=2 * size, transcendentals=0),
    )(*args)


def ring(axis, step):
    stride = 1 << SHIFT[axis]
    pairs = []
    for device in range(64):
        digit = device // stride % 4
        pairs.append((device, device + ((digit + step) % 4 - digit) * stride))
    return pairs


def swap_z(blocks):
    moved = {step: lax.ppermute(blocks[step], "tm", ring("z", step)) for step in (2, 1, 3)}
    return [blocks[0], moved[1], moved[2], moved[3]]


def swap_plane(value):
    groups = [[16 * x + 4 * y + z for x in range(4) for y in range(4)] for z in range(4)]
    return lax.all_to_all(
        value, "tm", split_axis=0, concat_axis=0, axis_index_groups=groups, tiled=True
    )


FWD = (16, 16, 1024)


def on_device(seed_field):
    table = tables()
    tm = lax.axis_index("tm")

    seed = seed_field.reshape(2, HOPS, HOP)
    last = seed_field[0, :, LOCAL - TAPS :].reshape(8, 128)
    last = lax.ppermute(last, "tm", [(d, (d + 1) % 64) for d in range(64)]).reshape(2, TAPS)
    spots = (tm * LOCAL - TAPS + jnp.arange(TAPS, dtype=jnp.int32)) & (NT - 1)
    halo = ((last[0] + pulse_of(spots)) ** 2 + last[1] ** 2)[None, :]

    value = call(
        start_kernel, [FWD],
        [(136, 1024), (128, 1024), pltpu.VMEM((2, 768, 256), BF16), pltpu.SemaphoreType.DMA],
        seed, halo, table["toeplitz"], specs=[VMEM, VMEM, HBM],
    )[0]
    value = swap_plane(value)
    blocks = call(fwd_kernel, [(4, 16, 1024)] * 4, [(4, 4, 16, 1024)], value)
    *blocks, late = lax.optimization_barrier((*blocks, tm))
    number = (
        (late % 4 + 4 * (late // 4 % 4) + 16 * (late // 16))
        + 8192 * jnp.arange(4, dtype=jnp.int32)[:, None, None]
        + 64 * jnp.arange(128, dtype=jnp.int32)[None, :, None]
        + 32768 * jnp.arange(256, dtype=jnp.int32)[None, None, :]
    ).reshape(512, 256)
    freq = jnp.where(number < NT // 2, number, number - NT)
    angle = (2.0 * math.pi / (1 << 28)) * (freq * freq & ((1 << 28) - 1)).astype(F32)
    disp = jnp.stack([jnp.cos(angle), jnp.sin(angle)])
    blocks = swap_z(blocks)
    *blocks, disp = lax.optimization_barrier((*blocks, disp))
    value = call(mid_kernel, [FWD], [], *blocks)[0]
    value = swap_plane(value)
    value = call(
        spectrum_kernel, [(16, 136, 128)],
        [(256, 1024), (512, 512), (512, 512), (1024, 256), (128, 256), (256, 128), (128, 128)],
        value, table["squares"], disp,
    )[0]
    value = swap_plane(value)
    blocks = call(unmid_kernel, [(528, 128)] * 4, [], value)
    blocks = swap_z(blocks)
    value, bins = call(inv_kernel, [(16, 136, 128), (8, 128)], [(4, 520, 128)], *blocks)
    value = swap_plane(value)

    alike = [bins] + [
        lax.ppermute(bins, "grp", [(g, (g + step) % 4) for g in range(4)]) for step in (1, 2, 3)
    ]
    normal, side = call(normal_kernel, [(4, 8, 128), (4, 256, 128)], [(128, 128)], *alike)
    columns = []
    for step in range(4):
        pairs = []
        for g in range(4):
            for d in range(64):
                x, y, z = d // 16, d // 4 % 4, d % 4
                pairs.append((g * 64 + d, x * 64 + g * 16 + (y + step) % 4 * 4 + z))
        columns.append(lax.ppermute(normal, ("grp", "tm"), pairs))

    spectrogram = call(
        frames_kernel, [(HOPS, W)], [(16, 256, 128), (HOPS, W), pltpu.SemaphoreType.DMA((4,))],
        value, table["frames"], place=HBM,
    )[0]
    spectrogram, side, *columns = lax.optimization_barrier((spectrogram, side, *columns))
    correlation = pl.pallas_call(
        correlation_kernel,
        grid=(4,),
        out_shape=jax.ShapeDtypeStruct((256, 4096), F32),
        in_specs=[pl.BlockSpec((4, 256, 128), lambda i: (0, 0, 0))]
        + [pl.BlockSpec((4, 8, 128), lambda i: (0, 0, 0))] * 4,
        out_specs=pl.BlockSpec((64, 4096), lambda i: (i, 0)),
        scratch_shapes=[pltpu.VMEM((4, 32, 128), F32)],
        compiler_params=PARAMS,
        cost_estimate=pl.CostEstimate(flops=1 << 23, bytes_accessed=1 << 22, transcendentals=0),
    )(side, *columns)
    return spectrogram[None], correlation


def solution(mesh):
    return jax.shard_map(
        on_device,
        mesh=mesh,
        in_specs=(P("grp", None, "tm"),),
        out_specs=(P("grp", "tm", None), P("tm", "grp")),
        check_vma=False,
    )
```

```python
import functools
import math

import jax
import jax.numpy as jnp
import ml_dtypes
import numpy as np
from jax import lax
from jax.experimental import pallas as pl
from jax.experimental.pallas import tpu as pltpu
from jax.sharding import PartitionSpec as P

NT = 1 << 23
LOCAL = 1 << 17
HOPS = 128
HOP = 1024
W = 2048
BINS = 16384
TAPS = 512
BIN_WIDTH = 512
PEAK_AMPLITUDE = 2.0
KERR_GAIN = 0.5
RAMAN_SHARE = 0.18
RESPONSE_FAST = 12.2
RESPONSE_SLOW = 32.0
RESPONSE_SCALE = (12.2 * 12.2 + 32.0 * 32.0) / (12.2 * 32.0 * 32.0)
FLOOR_SHARE = 0.5
F32 = jnp.float32
BF16 = jnp.bfloat16
VMEM = pl.BlockSpec(memory_space=pltpu.VMEM)
HBM = pl.BlockSpec(memory_space=pltpu.HBM)
PARAMS = pltpu.CompilerParams(vmem_limit_bytes=24 << 20)


def split_const(table):
    table = np.asarray(table, np.float64)
    high = table.astype(ml_dtypes.bfloat16)
    low = (table - high.astype(np.float64)).astype(ml_dtypes.bfloat16)
    return np.stack([high, low])


def left_form(matrix):
    return np.block([[matrix.real, -matrix.imag], [matrix.imag, matrix.real]])


def right_form(matrix):
    return np.block([[matrix.real, matrix.imag], [-matrix.imag, matrix.real]])


def dft(size, sign):
    index = np.arange(size)
    return np.exp(sign * 2j * np.pi * (index[:, None] * index[None, :] % size) / size)


def row_order():
    row = np.arange(256)
    return row // 16 + 16 * (row % 16)


@functools.lru_cache(maxsize=None)
def tables():
    out = {}
    lag = np.arange(256)[None, :] - np.arange(256)[:, None]
    taps = np.arange(TAPS)
    response = RESPONSE_SCALE * np.exp(-taps / RESPONSE_SLOW) * np.sin(taps / RESPONSE_FAST)
    blocks = []
    for step in range(3):
        position = 256 * step + lag
        inside = (position >= 0) & (position < TAPS)
        blocks.append(np.where(inside, response[np.clip(position, 0, TAPS - 1)], 0.0))
    out["toeplitz"] = split_const(np.concatenate(blocks, 0))
    rows = np.arange(256).reshape(2, 16, 8).transpose(1, 0, 2).reshape(256)
    forward = dft(256, -1)
    inverse = dft(256, 1)[row_order()] / NT
    squares = [left_form(dft(128, -1))[:, rows], right_form(dft(128, 1))]
    squares += [forward.real, forward.imag, inverse.real, inverse.imag]
    out["squares"] = np.concatenate([split_const(square) for square in squares])
    order = np.arange(256).reshape(2, 2, 64).transpose(1, 0, 2).reshape(256)
    out["frames"] = split_const(left_form(dft(128, -1))[:, order])
    return out


def halves(value):
    high = value.astype(BF16)
    low = (value - high.astype(F32)).astype(BF16)
    return high, low


def dims(contract):
    return (contract, ((), ()))


NN = ((1,), (0,))
NT_FORM = ((1,), (1,))


def dot_right(values, tables):
    left, right = [], []
    for value, table in zip(values, tables):
        high, low = halves(value)
        left += [low, high, high]
        right += [table[0], table[1], table[0]]
    left, right = jnp.concatenate(left, axis=1), jnp.concatenate(right, axis=0)
    return jnp.dot(left, right, preferred_element_type=F32)


def dot_left(tables, values, contract=NN):
    left, right = [], []
    for value, table in zip(values, tables):
        high, low = halves(value)
        left += [table[0], table[1], table[0]]
        right += [low, high, high]
    left, right = jnp.concatenate(left, axis=1), jnp.concatenate(right, axis=contract[1][0])
    return lax.dot_general(left, right, dims(contract), preferred_element_type=F32)


def cmul(a, b):
    return (a[0] * b[0] - a[1] * b[1], a[0] * b[1] + a[1] * b[0])


def quad(x, sign):
    s02 = (x[0][0] + x[2][0], x[0][1] + x[2][1])
    d02 = (x[0][0] - x[2][0], x[0][1] - x[2][1])
    s13 = (x[1][0] + x[3][0], x[1][1] + x[3][1])
    d13 = (x[1][0] - x[3][0], x[1][1] - x[3][1])
    turned = (-sign * d13[1], sign * d13[0])
    return [
        (s02[0] + s13[0], s02[1] + s13[1]),
        (d02[0] + turned[0], d02[1] + turned[1]),
        (s02[0] - s13[0], s02[1] - s13[1]),
        (d02[0] - turned[0], d02[1] - turned[1]),
    ]


def powers(first):
    second = (first[0] * first[0] - first[1] * first[1], 2.0 * first[0] * first[1])
    return [None, first, second, cmul(first, second)]


def twist(values, factors):
    return [values[0]] + [cmul(values[k], factors[k]) for k in (1, 2, 3)]


def sincos(x):
    turns = jnp.floor(x * (2.0 / math.pi) + 0.5)
    rest = ((x - turns * 1.5703125) - turns * 4.837512969970703125e-4) - turns * 7.549789948768648e-8
    sq = rest * rest
    sine = rest + rest * sq * (
        -1.6666654611e-1 + sq * (8.3321608736e-3 + sq * -1.9515295891e-4)
    )
    cosine = 1.0 - 0.5 * sq + sq * sq * (
        4.166664568298827e-2 + sq * (-1.388731625493765e-3 + sq * 2.443315711809948e-5)
    )
    part = turns.astype(jnp.int32)
    odd = (part & 1) == 1
    s_val = jnp.where(odd, cosine, sine)
    c_val = jnp.where(odd, sine, cosine)
    s_val = jnp.where((part & 2) == 2, -s_val, s_val)
    c_val = jnp.where(((part + 1) & 2) == 2, -c_val, c_val)
    return s_val, c_val


def pulse_of(position):
    offset = (position - NT // 2).astype(F32) * (16.0 / NT)
    fall = jnp.exp(-jnp.abs(offset))
    return (2.0 * PEAK_AMPLITUDE) * fall / (1.0 + fall * fall)


SHIFT = {"x": 4, "y": 2, "z": 0}


def digits():
    tm = lax.axis_index("tm")
    return {axis: (tm >> SHIFT[axis]) & 3 for axis in SHIFT}


def iota(shape, axis):
    return lax.broadcasted_iota(jnp.int32, shape, axis)


def phasor(number, span, sign):
    sine, cosine = sincos((sign * 2.0 * math.pi / span) * number.astype(F32))
    return cosine, sine


def turn(number, span, sign):
    angle = sign * 2.0 * math.pi * number / span
    return math.cos(angle), math.sin(angle)


def eight(start):
    return pl.ds(pl.multiple_of(start, 8), 8)


def start_kernel(seed, halo, toep_hbm, out, buf, fre, toep, sem):
    copy = pltpu.make_async_copy(toep_hbm, toep, sem)
    copy.start()
    base = lax.axis_index("tm") * LOCAL
    buf[0:8, 512:1024] = jnp.broadcast_to(halo[...], (8, 512))

    def fill(step, carry):
        rows = eight(step * 8)
        row = iota((8, 1024), 0) + step * 8
        value = seed[0, rows, :] + pulse_of(base + row * 1024 + iota((8, 1024), 1))
        other = seed[1, rows, :]
        fre[rows, :] = value
        buf[eight(step * 8 + 8), :] = value * value + other * other
        return carry

    lax.fori_loop(0, 16, fill, 0, unroll=4)
    copy.wait()
    own = [halves(buf[8:136, 256 * e : 256 * e + 256]) for e in range(4)]
    back = {e: halves(buf[7:135, 256 * e : 256 * e + 256]) for e in (2, 3)}
    for e in range(4):
        left, right = [], []
        for step in range(3):
            at = e - step
            high, low = own[at] if at >= 0 else back[at + 4]
            rows = slice(256 * step, 256 * step + 256)
            left += [low, high, high]
            right += [toep[0, rows, :], toep[1, rows, :], toep[0, rows, :]]
        left, right = jnp.concatenate(left, axis=1), jnp.concatenate(right, axis=0)
        total = jnp.dot(left, right, preferred_element_type=F32)
        lanes = slice(256 * e, 256 * e + 256)
        phase = KERR_GAIN * ((1.0 - RAMAN_SHARE) * buf[8:136, lanes] + RAMAN_SHARE * total)
        sine, cosine = sincos(phase)
        value = fre[:, lanes]
        other = seed[1, :, lanes]
        out[:, 0:8, lanes] = (value * cosine - other * sine).reshape(16, 8, 256)
        out[:, 8:16, lanes] = (value * sine + other * cosine).reshape(16, 8, 256)


def sixteen(x, sign):
    inner = [quad([x[4 * a1 + a0] for a1 in range(4)], sign) for a0 in range(4)]
    out = []
    for c0 in range(4):
        row = [inner[a0][c0] for a0 in range(4)]
        row = [cmul(v, turn(a0 * c0, 16, sign)) if a0 * c0 else v for a0, v in enumerate(row)]
        out.append(quad(row, sign))
    return out


def many_powers(first):
    out = [None, first]
    for k in range(2, 16):
        out.append(cmul(out[k // 2], out[k - k // 2]))
    return out


def lanes_at(step):
    return pl.ds(pl.multiple_of(step * 128, 128), 128)


def fwd_kernel(blocks, o0, o1, o2, o3, scratch):
    place = digits()
    block = 4 * place["x"] + place["y"]
    number = place["z"] * LOCAL + (8 * block + iota((8, 128), 0)) * 1024 + iota((8, 128), 1)
    forward = turn(128, NT, -1)

    def body(step, factor):
        lanes = lanes_at(step)
        y = sixteen([(blocks[t, 0:8, lanes], blocks[t, 8:16, lanes]) for t in range(16)], -1.0)
        factors = many_powers(factor)
        for c0 in range(4):
            slot = (c0 - place["z"]) & 3
            for c1 in range(4):
                value = y[c0][c1]
                if c0 + c1:
                    value = cmul(value, factors[c0 + 4 * c1])
                scratch[slot, c1, 0:8, lanes] = value[0]
                scratch[slot, c1, 8:16, lanes] = value[1]
        for j, out in enumerate((o0, o1, o2, o3)):
            out[:, :, lanes] = scratch[j, :, :, lanes]
        return cmul(factor, forward)

    lax.fori_loop(0, 8, body, phasor(number, NT, -1), unroll=4)


def mid_kernel(r0, r1, r2, r3, out):
    place = digits()
    block = 4 * place["x"] + place["y"]
    number = (8 * block + iota((8, 128), 0)) * 1024 + iota((8, 128), 1) + place["z"] * LOCAL
    forward = turn(128, 4 * LOCAL, -1)

    def body(step, factor):
        lanes = lanes_at(step)
        factors = powers(factor)
        for kk in range(4):
            x = [(r[kk, 0:8, lanes], r[kk, 8:16, lanes]) for r in (r0, r1, r2, r3)]
            for ka, value in enumerate(twist(quad(x, 1.0), factors)):
                out[4 * ka + kk, 0:8, lanes] = value[0]
                out[4 * ka + kk, 8:16, lanes] = value[1]
        return cmul(factor, forward)

    lax.fori_loop(0, 8, body, phasor(number, 4 * LOCAL, -1), unroll=4)


def spectrum_kernel(blocks, squares, disp, out, wide, work, back, rows_w, bins, flip, flat):
    hop, unhop = squares.at[0:2], squares.at[2:4]
    fwd_c, fwd_s, inv_c, inv_s = [squares.at[2 * k : 2 * k + 2] for k in range(2, 6)]
    for part in range(4):
        lanes = slice(256 * part, 256 * part + 256)
        wide[:, lanes] = dot_left([hop], [blocks[:, :, lanes].reshape(256, 256)])
    lane_f = powers(phasor(iota((8, 256), 1), 1024, -1))
    number = [256 * part + iota((8, 256), 1) for part in range(4)]
    cross_first = tuple(phasor(iota((8, 256), 0) * n, LOCAL, -1) for n in number)
    cross_step = [phasor(8 * n, LOCAL, -1) for n in number]

    def body(step, carry):
        rows, low_rows = eight(step * 8), eight(step * 8 + 128)
        x = []
        for part in range(4):
            lanes = slice(256 * part, 256 * part + 256)
            x.append(cmul((wide[rows, lanes], wide[low_rows, lanes]), carry[part]))
        y = twist(quad(x, -1.0), lane_f)
        for k in range(4):
            at = eight(step * 8 + 128 * k)
            work[at, 0:256] = y[k][0]
            work[at, 256:512] = y[k][1]
        return tuple(cmul(value, move) for value, move in zip(carry, cross_step))

    lax.fori_loop(0, 16, body, cross_first, unroll=4)
    bins[64:128, :] = jnp.zeros((64, 256), F32)
    for k in range(4):
        rows = slice(128 * k, 128 * k + 128)
        re, im = work[rows, 0:256], work[rows, 256:512]
        re, im = dot_right([re, -im], [fwd_c, fwd_s]), dot_right([re, im], [fwd_s, fwd_c])
        power = (re * re + im * im).reshape(16, 8, 256)
        bins[16 * k : 16 * k + 16, :] = jnp.sum(power, axis=1) * (1.0 / (NT * BIN_WIDTH))
        re, im = cmul((re, im), (disp[0, rows, :], disp[1, rows, :]))
        work[rows, 0:256] = re
        work[rows, 256:512] = im
    for half in range(2):
        flip[128 * half : 128 * half + 128, :] = bins[:, 128 * half : 128 * half + 128].T
    flat[...] = flip[pl.ds(0, 128, stride=2), :] + pltpu.roll(flip[pl.ds(1, 128, stride=2), :], 64, 1)
    for dest in range(16):
        out[dest, 128:136, :] = flat[8 * dest : 8 * dest + 8, :]
    re, im = work[:, 0:256], work[:, 256:512]
    back[0:256, :] = dot_left([inv_c, inv_s], [re, -im], NT_FORM)
    back[256:512, :] = dot_left([inv_s, inv_c], [re, im], NT_FORM)
    first = phasor(16 * iota((8, 128), 0), 1024, 1)
    forward, half_turn = turn(1, 1024, 1), turn(128, 1024, 1)
    freq = iota((8, 128), 1)
    cross_first = phasor(16 * iota((8, 128), 0) * freq, LOCAL, 1)
    cross_step, cross_half = phasor(freq, LOCAL, 1), phasor(128 * freq, LOCAL, 1)
    cross_part = powers(phasor(256 * freq, LOCAL, 1))

    def tail(a, carry):
        factor, other = carry
        for half in range(2):
            rows, low_rows = eight(a * 16 + 8 * half), eight(a * 16 + 8 * half + 256)
            x = [
                (back[rows, 128 * k : 128 * k + 128], back[low_rows, 128 * k : 128 * k + 128])
                for k in range(4)
            ]
            now = cmul(factor, half_turn) if half else factor
            after = cmul(other, cross_half) if half else other
            y = twist(quad(twist(x, powers(now)), 1.0), cross_part)
            for part in range(4):
                value = cmul(y[part], after)
                at = eight(a * 64 + part * 16 + 8 * half)
                rows_w[at, 0:128] = value[0]
                rows_w[at, 128:256] = value[1]
        return cmul(factor, forward), cmul(other, cross_step)

    lax.fori_loop(0, 16, tail, (first, cross_first), unroll=4)
    for part in range(4):
        got = dot_right([rows_w[256 * part : 256 * part + 256, :]], [unhop])
        for a in range(4):
            out[4 * part + a, 0:64, :] = got[64 * a : 64 * a + 64, 0:128]
            out[4 * part + a, 64:128, :] = got[64 * a : 64 * a + 64, 128:256]


def unmid_kernel(blocks, o0, o1, o2, o3):
    place = digits()
    outs = (o0, o1, o2, o3)
    total = blocks[0, 128:136, :]
    for k in range(1, 16):
        total = total + blocks[k, 128:136, :]
    for out in outs:
        out[520:528, :] = total
    block = 4 * place["x"] + place["y"]
    number = block + 16 * iota((8, 128), 0) + 1024 * iota((8, 128), 1) + place["z"] * LOCAL
    forward = turn(128, 4 * LOCAL, 1)

    def body(step, factor):
        rows, low_rows = eight(step * 8), eight(step * 8 + 64)
        factors = powers(factor)
        for kk in range(4):
            x = [(blocks[4 * ka + kk, rows, :], blocks[4 * ka + kk, low_rows, :]) for ka in range(4)]
            for out, value in zip(outs, quad(twist(x, factors), 1.0)):
                out[eight(step * 8 + 128 * kk), :] = value[0]
                out[eight(step * 8 + 128 * kk + 64), :] = value[1]
        return cmul(factor, forward)

    lax.fori_loop(0, 8, body, phasor(number, 4 * LOCAL, 1), unroll=4)
    pick = jnp.where(iota((16, 128), 1) == 0, 1.0, 0.0).astype(BF16)
    for j in range(4):
        high, low = halves(outs[(j + 1) % 4][0:512, :])
        row = lax.dot_general(pick, high, dims(NT_FORM), preferred_element_type=F32)
        row = row + lax.dot_general(pick, low, dims(NT_FORM), preferred_element_type=F32)
        for kk in range(4):
            outs[j][512 + kk : 513 + kk, :] = row[0:1, 128 * kk : 128 * kk + 128]
        outs[j][516:520, :] = jnp.zeros((4, 128), F32)


def unsixteen(x, factors):
    line = [None] * 16
    for c0 in range(4):
        for c1 in range(4):
            value = x[c0][c1]
            line[4 * c1 + c0] = cmul(value, factors[c0 + 4 * c1]) if c0 + c1 else value
    return sixteen(line, 1.0)


def inv_kernel(r0, r1, r2, r3, out, bins, blocks):
    place = digits()
    bins[...] = (r0[520:528, :] + r1[520:528, :]) + (r2[520:528, :] + r3[520:528, :])
    for s, value in enumerate((r0, r1, r2, r3)):
        blocks[(place["z"] - s) & 3] = value[0:520, :]
    block = 4 * place["x"] + place["y"]
    number = place["z"] * LOCAL + block + 16 * iota((8, 128), 0) + 1024 * iota((8, 128), 1)
    forward = turn(128, NT, 1)

    def body(step, factor):
        x = [
            [
                (blocks[c0, eight(step * 8 + 128 * c1), :], blocks[c0, eight(step * 8 + 128 * c1 + 64), :])
                for c1 in range(4)
            ]
            for c0 in range(4)
        ]
        y = unsixteen(x, many_powers(factor))
        for a0 in range(4):
            for a1 in range(4):
                out[4 * a1 + a0, eight(step * 8), :] = y[a0][a1][0]
                out[4 * a1 + a0, eight(step * 8 + 64), :] = y[a0][a1][1]
        return cmul(factor, forward)

    lax.fori_loop(0, 8, body, phasor(number, NT, 1), unroll=4)
    after = (place["z"] + 1) & 3
    lane = iota((8, 128), 1)
    factors = many_powers(phasor(after * LOCAL + block + 16 * (lane & 63), NT, 1))
    x = []
    for c0 in range(4):
        rows = [
            jnp.broadcast_to(blocks[c0, 512 + c1 : 513 + c1, :], (8, 128)) for c1 in range(4)
        ]
        x.append([(row, pltpu.roll(row, 64, 1)) for row in rows])
    y = unsixteen(x, factors)
    flat = []
    for t in range(16):
        re, im = y[t % 4][t // 4]
        flat.append(jnp.where(lane < 64, re, pltpu.roll(im, 64, 1)))
    wrap = after == 0
    for t in range(16):
        out[t, 128:136, :] = jnp.where(wrap, flat[(t + 1) % 16], flat[t])


def frames_kernel(blocks, mat, out_hbm, got, out, sems):
    columns = jnp.concatenate([blocks[a, 128:129, :] for a in range(16)], axis=0).T
    lane = iota((128, 128), 1)
    wave = phasor(16 * iota((64, 128), 0), W, 1)
    for a in range(16):
        here = blocks[a, 0:128, :]
        after = jnp.where(lane == 127, columns[:, a : a + 1], pltpu.roll(here, 127, 1))
        late = 0.5 + 0.5 * wave[0]
        early = 0.5 - 0.5 * wave[0]
        pieces = [here[0:64] * early, here[64:128] * early, after[0:64] * late, after[64:128] * late]
        got[a] = dot_left([mat], [jnp.concatenate(pieces, axis=0)])
        wave = cmul(wave, turn(1, W, 1))
    first = phasor(iota((8, 128), 0), W, -1)
    forward = turn(8, W, -1)

    def body(step, factor):
        rows, low_rows = eight(step * 8), eight(step * 8 + 128)
        factors = many_powers(factor)
        x = [(got[a, rows, :], got[a, low_rows, :]) for a in range(16)]
        y = sixteen([cmul(x[a], factors[a]) if a else x[a] for a in range(16)], -1.0)
        for c0 in range(4):
            for c1 in range(4):
                value = y[c0][c1]
                got[c0 + 4 * c1, rows, :] = (value[0] * value[0] + value[1] * value[1]) * (1.0 / W)
        return cmul(factor, forward)

    lax.fori_loop(0, 16, body, first, unroll=4)
    copies = []
    for c in range(16):
        out[:, 128 * c : 128 * c + 128] = got[c, 0:128, :].T
        if c % 4 == 3:
            lanes = pl.ds(128 * (c - 3), 512)
            copies.append(pltpu.make_async_copy(out.at[:, lanes], out_hbm.at[:, lanes], sems.at[c // 4]))
            copies[-1].start()
    for copy in copies:
        copy.wait()


def normal_kernel(b0, b1, b2, b3, out, side, pad):
    blocks = [b[...] for b in (b0, b1, b2, b3)]
    total = (blocks[0] + blocks[1]) + (blocks[2] + blocks[3])
    average = total * 0.25
    centred = [b - average for b in blocks]
    sq = [c * c for c in centred]
    variance = ((sq[0] + sq[1]) + (sq[2] + sq[3])) * 0.25
    spread = jnp.sqrt(jnp.maximum(variance, FLOOR_SHARE * average * average / BIN_WIDTH))
    grp = lax.axis_index("grp")
    for step in range(4):
        out[(grp - step) & 3] = centred[step] / spread
    at = digits()["z"] * 2
    pad[...] = jnp.zeros((128, 128), F32)
    for r in range(4):
        for half in range(2):
            pad[2 * r + half : 2 * r + half + 1, :] = out[r, pl.ds(at + half, 1), :] * 0.25
    flipped = pad[...].T
    for r in range(4):
        for half in range(2):
            column = flipped[:, 2 * r + half : 2 * r + half + 1]
            side[r, 128 * half : 128 * half + 128, :] = jnp.broadcast_to(column, (128, 128))


def correlation_kernel(side, c0, c1, c2, c3, out, cols):
    step = pl.program_id(0)

    @pl.when(step == 0)
    def _():
        place = digits()
        for s, value in enumerate((c0, c1, c2, c3)):
            cols[:, eight(((place["y"] - s) & 3) * 8), :] = value[...]

    for half in range(2):
        base = 32 * half
        factors = [[side[r, eight(step * 64 + base + g * 8), :] for r in range(4)] for g in range(4)]
        for k in range(32):
            line = [jnp.broadcast_to(cols[r, k : k + 1, :], (8, 128)) for r in range(4)]
            for g in range(4):
                total = (factors[g][0] * line[0] + factors[g][1] * line[1]) + (
                    factors[g][2] * line[2] + factors[g][3] * line[3]
                )
                at = base + 8 * g
                out[at : at + 8, 128 * k : 128 * k + 128] = total


def call(kernel, outs, scratch, *args, flops=1 << 20, specs=None, place=VMEM):
    size = sum(int(np.prod(s)) * 4 for s in outs)
    return pl.pallas_call(
        kernel,
        out_shape=[jax.ShapeDtypeStruct(s, F32) for s in outs],
        in_specs=specs or [VMEM] * len(args),
        out_specs=[place] * len(outs),
        scratch_shapes=[pltpu.VMEM(s, F32) if isinstance(s, tuple) else s for s in scratch],
        compiler_params=PARAMS,
        cost_estimate=pl.CostEstimate(flops=flops, bytes_accessed=2 * size, transcendentals=0),
    )(*args)


def ring(axis, step):
    stride = 1 << SHIFT[axis]
    pairs = []
    for device in range(64):
        digit = device // stride % 4
        pairs.append((device, device + ((digit + step) % 4 - digit) * stride))
    return pairs


def swap_z(blocks):
    moved = {step: lax.ppermute(blocks[step], "tm", ring("z", step)) for step in (2, 1, 3)}
    return [blocks[0], moved[1], moved[2], moved[3]]


def swap_plane(value):
    groups = [[16 * x + 4 * y + z for x in range(4) for y in range(4)] for z in range(4)]
    return lax.all_to_all(
        value, "tm", split_axis=0, concat_axis=0, axis_index_groups=groups, tiled=True
    )


FWD = (16, 16, 1024)


def on_device(seed_field):
    table = tables()
    tm = lax.axis_index("tm")

    seed = seed_field.reshape(2, HOPS, HOP)
    last = seed_field[0, :, LOCAL - TAPS :].reshape(8, 128)
    last = lax.ppermute(last, "tm", [(d, (d + 1) % 64) for d in range(64)]).reshape(2, TAPS)
    spots = (tm * LOCAL - TAPS + jnp.arange(TAPS, dtype=jnp.int32)) & (NT - 1)
    halo = ((last[0] + pulse_of(spots)) ** 2 + last[1] ** 2)[None, :]

    value = call(
        start_kernel, [FWD],
        [(136, 1024), (128, 1024), pltpu.VMEM((2, 768, 256), BF16), pltpu.SemaphoreType.DMA],
        seed, halo, table["toeplitz"], specs=[VMEM, VMEM, HBM],
    )[0]
    value = swap_plane(value)
    blocks = call(fwd_kernel, [(4, 16, 1024)] * 4, [(4, 4, 16, 1024)], value)
    *blocks, late = lax.optimization_barrier((*blocks, tm))
    row = lax.broadcasted_iota(jnp.int32, (512, 256), 0)
    number = (
        (late % 4 + 4 * (late // 4 % 4) + 16 * (late // 16))
        + 64 * (row & 127)
        + 8192 * (row >> 7)
        + 32768 * late
        + 32768 * (lax.broadcasted_iota(jnp.int32, (512, 256), 1) - late)
    )
    freq = jnp.where(number < NT // 2, number, number - NT)
    angle = (2.0 * math.pi / (1 << 28)) * (freq * freq & ((1 << 28) - 1)).astype(F32)
    disp = jnp.stack([jnp.cos(angle), jnp.sin(angle)])
    blocks = swap_z(blocks)
    *blocks, disp = lax.optimization_barrier((*blocks, disp))
    value = call(mid_kernel, [FWD], [], *blocks)[0]
    value = swap_plane(value)
    value = call(
        spectrum_kernel, [(16, 136, 128)],
        [(256, 1024), (512, 512), (512, 512), (1024, 256), (128, 256), (256, 128), (128, 128)],
        value, table["squares"], disp,
    )[0]
    value = swap_plane(value)
    blocks = call(unmid_kernel, [(528, 128)] * 4, [], value)
    blocks = swap_z(blocks)
    value, bins = call(inv_kernel, [(16, 136, 128), (8, 128)], [(4, 520, 128)], *blocks)
    value = swap_plane(value)

    alike = [bins] + [
        lax.ppermute(bins, "grp", [(g, (g + step) % 4) for g in range(4)]) for step in (1, 2, 3)
    ]
    normal, side = call(normal_kernel, [(4, 8, 128), (4, 256, 128)], [(128, 128)], *alike)
    columns = []
    for step in range(4):
        pairs = []
        for g in range(4):
            for d in range(64):
                x, y, z = d // 16, d // 4 % 4, d % 4
                pairs.append((g * 64 + d, x * 64 + g * 16 + (y + step) % 4 * 4 + z))
        columns.append(lax.ppermute(normal, ("grp", "tm"), pairs))

    spectrogram = call(
        frames_kernel, [(HOPS, W)], [(16, 256, 128), (HOPS, W), pltpu.SemaphoreType.DMA((4,))],
        value, table["frames"], place=HBM,
    )[0]
    spectrogram, side, *columns = lax.optimization_barrier((spectrogram, side, *columns))
    correlation = pl.pallas_call(
        correlation_kernel,
        grid=(4,),
        out_shape=jax.ShapeDtypeStruct((256, 4096), F32),
        in_specs=[pl.BlockSpec((4, 256, 128), lambda i: (0, 0, 0))]
        + [pl.BlockSpec((4, 8, 128), lambda i: (0, 0, 0))] * 4,
        out_specs=pl.BlockSpec((64, 4096), lambda i: (i, 0)),
        scratch_shapes=[pltpu.VMEM((4, 32, 128), F32)],
        compiler_params=PARAMS,
        cost_estimate=pl.CostEstimate(flops=1 << 23, bytes_accessed=1 << 22, transcendentals=0),
    )(side, *columns)
    return spectrogram[None], correlation


def solution(mesh):
    return jax.shard_map(
        on_device,
        mesh=mesh,
        in_specs=(P("grp", None, "tm"),),
        out_specs=(P("grp", "tm", None), P("tm", "grp")),
        check_vma=False,
    )
```

```python
import functools
import math

import jax
import jax.numpy as jnp
import ml_dtypes
import numpy as np
from jax import lax
from jax.experimental import pallas as pl
from jax.experimental.pallas import tpu as pltpu
from jax.sharding import PartitionSpec as P

NT = 1 << 23
LOCAL = 1 << 17
HOPS = 128
HOP = 1024
W = 2048
BINS = 16384
TAPS = 512
BIN_WIDTH = 512
PEAK_AMPLITUDE = 2.0
KERR_GAIN = 0.5
RAMAN_SHARE = 0.18
RESPONSE_FAST = 12.2
RESPONSE_SLOW = 32.0
RESPONSE_SCALE = (12.2 * 12.2 + 32.0 * 32.0) / (12.2 * 32.0 * 32.0)
FLOOR_SHARE = 0.5
F32 = jnp.float32
BF16 = jnp.bfloat16
VMEM = pl.BlockSpec(memory_space=pltpu.VMEM)
HBM = pl.BlockSpec(memory_space=pltpu.HBM)
PARAMS = pltpu.CompilerParams(vmem_limit_bytes=24 << 20)


def split_const(table):
    table = np.asarray(table, np.float64)
    high = table.astype(ml_dtypes.bfloat16)
    low = (table - high.astype(np.float64)).astype(ml_dtypes.bfloat16)
    return np.stack([high, low])


def left_form(matrix):
    return np.block([[matrix.real, -matrix.imag], [matrix.imag, matrix.real]])


def right_form(matrix):
    return np.block([[matrix.real, matrix.imag], [-matrix.imag, matrix.real]])


def dft(size, sign):
    index = np.arange(size)
    return np.exp(sign * 2j * np.pi * (index[:, None] * index[None, :] % size) / size)


def row_order():
    row = np.arange(256)
    return row // 16 + 16 * (row % 16)


@functools.lru_cache(maxsize=None)
def tables():
    out = {}
    lag = np.arange(256)[None, :] - np.arange(256)[:, None]
    taps = np.arange(TAPS)
    response = RESPONSE_SCALE * np.exp(-taps / RESPONSE_SLOW) * np.sin(taps / RESPONSE_FAST)
    blocks = []
    for step in range(3):
        position = 256 * step + lag
        inside = (position >= 0) & (position < TAPS)
        blocks.append(np.where(inside, response[np.clip(position, 0, TAPS - 1)], 0.0))
    out["toeplitz"] = split_const(np.concatenate(blocks, 0))
    rows = np.arange(256).reshape(2, 16, 8).transpose(1, 0, 2).reshape(256)
    forward = dft(256, -1)
    inverse = dft(256, 1)[row_order()] / NT
    squares = [left_form(dft(128, -1))[:, rows], right_form(dft(128, 1))]
    squares += [forward.real, forward.imag, inverse.real, inverse.imag]
    out["squares"] = np.concatenate([split_const(square) for square in squares])
    order = np.arange(256).reshape(2, 2, 64).transpose(1, 0, 2).reshape(256)
    out["frames"] = split_const(left_form(dft(128, -1))[:, order])
    return out


def halves(value):
    high = value.astype(BF16)
    low = (value - high.astype(F32)).astype(BF16)
    return high, low


def dims(contract):
    return (contract, ((), ()))


NN = ((1,), (0,))
NT_FORM = ((1,), (1,))


def dot_right(values, tables):
    left, right = [], []
    for value, table in zip(values, tables):
        high, low = halves(value)
        left += [low, high, high]
        right += [table[0], table[1], table[0]]
    left, right = jnp.concatenate(left, axis=1), jnp.concatenate(right, axis=0)
    return jnp.dot(left, right, preferred_element_type=F32)


def dot_left(tables, values, contract=NN):
    left, right = [], []
    for value, table in zip(values, tables):
        high, low = halves(value)
        left += [table[0], table[1], table[0]]
        right += [low, high, high]
    left, right = jnp.concatenate(left, axis=1), jnp.concatenate(right, axis=contract[1][0])
    return lax.dot_general(left, right, dims(contract), preferred_element_type=F32)


def cmul(a, b):
    return (a[0] * b[0] - a[1] * b[1], a[0] * b[1] + a[1] * b[0])


def quad(x, sign):
    s02 = (x[0][0] + x[2][0], x[0][1] + x[2][1])
    d02 = (x[0][0] - x[2][0], x[0][1] - x[2][1])
    s13 = (x[1][0] + x[3][0], x[1][1] + x[3][1])
    d13 = (x[1][0] - x[3][0], x[1][1] - x[3][1])
    turned = (-sign * d13[1], sign * d13[0])
    return [
        (s02[0] + s13[0], s02[1] + s13[1]),
        (d02[0] + turned[0], d02[1] + turned[1]),
        (s02[0] - s13[0], s02[1] - s13[1]),
        (d02[0] - turned[0], d02[1] - turned[1]),
    ]


def powers(first):
    second = (first[0] * first[0] - first[1] * first[1], 2.0 * first[0] * first[1])
    return [None, first, second, cmul(first, second)]


def twist(values, factors):
    return [values[0]] + [cmul(values[k], factors[k]) for k in (1, 2, 3)]


def sincos(x):
    turns = jnp.floor(x * (2.0 / math.pi) + 0.5)
    rest = ((x - turns * 1.5703125) - turns * 4.837512969970703125e-4) - turns * 7.549789948768648e-8
    sq = rest * rest
    sine = rest + rest * sq * (
        -1.6666654611e-1 + sq * (8.3321608736e-3 + sq * -1.9515295891e-4)
    )
    cosine = 1.0 - 0.5 * sq + sq * sq * (
        4.166664568298827e-2 + sq * (-1.388731625493765e-3 + sq * 2.443315711809948e-5)
    )
    part = turns.astype(jnp.int32)
    odd = (part & 1) == 1
    s_val = jnp.where(odd, cosine, sine)
    c_val = jnp.where(odd, sine, cosine)
    s_val = jnp.where((part & 2) == 2, -s_val, s_val)
    c_val = jnp.where(((part + 1) & 2) == 2, -c_val, c_val)
    return s_val, c_val


def pulse_of(position):
    offset = (position - NT // 2).astype(F32) * (16.0 / NT)
    fall = jnp.exp(-jnp.abs(offset))
    return (2.0 * PEAK_AMPLITUDE) * fall / (1.0 + fall * fall)


SHIFT = {"x": 4, "y": 2, "z": 0}


def digits():
    tm = lax.axis_index("tm")
    return {axis: (tm >> SHIFT[axis]) & 3 for axis in SHIFT}


def iota(shape, axis):
    return lax.broadcasted_iota(jnp.int32, shape, axis)


def phasor(number, span, sign):
    sine, cosine = sincos((sign * 2.0 * math.pi / span) * number.astype(F32))
    return cosine, sine


def turn(number, span, sign):
    angle = sign * 2.0 * math.pi * number / span
    return math.cos(angle), math.sin(angle)


def eight(start):
    return pl.ds(pl.multiple_of(start, 8), 8)


def start_kernel(seed, halo, toep_hbm, out, buf, fre, toep, sem):
    copy = pltpu.make_async_copy(toep_hbm, toep, sem)
    copy.start()
    base = lax.axis_index("tm") * LOCAL
    buf[0:8, 512:1024] = jnp.broadcast_to(halo[...], (8, 512))

    def fill(step, carry):
        rows = eight(step * 8)
        row = iota((8, 1024), 0) + step * 8
        value = seed[0, rows, :] + pulse_of(base + row * 1024 + iota((8, 1024), 1))
        other = seed[1, rows, :]
        fre[rows, :] = value
        buf[eight(step * 8 + 8), :] = value * value + other * other
        return carry

    lax.fori_loop(0, 16, fill, 0, unroll=4)
    copy.wait()
    own = [halves(buf[8:136, 256 * e : 256 * e + 256]) for e in range(4)]
    back = {e: halves(buf[7:135, 256 * e : 256 * e + 256]) for e in (2, 3)}
    for e in range(4):
        left, right = [], []
        for step in range(3):
            at = e - step
            high, low = own[at] if at >= 0 else back[at + 4]
            rows = slice(256 * step, 256 * step + 256)
            left += [low, high, high]
            right += [toep[0, rows, :], toep[1, rows, :], toep[0, rows, :]]
        left, right = jnp.concatenate(left, axis=1), jnp.concatenate(right, axis=0)
        total = jnp.dot(left, right, preferred_element_type=F32)
        lanes = slice(256 * e, 256 * e + 256)
        phase = KERR_GAIN * ((1.0 - RAMAN_SHARE) * buf[8:136, lanes] + RAMAN_SHARE * total)
        sine, cosine = sincos(phase)
        value = fre[:, lanes]
        other = seed[1, :, lanes]
        out[:, 0:8, lanes] = (value * cosine - other * sine).reshape(16, 8, 256)
        out[:, 8:16, lanes] = (value * sine + other * cosine).reshape(16, 8, 256)


def sixteen(x, sign):
    inner = [quad([x[4 * a1 + a0] for a1 in range(4)], sign) for a0 in range(4)]
    out = []
    for c0 in range(4):
        row = [inner[a0][c0] for a0 in range(4)]
        row = [cmul(v, turn(a0 * c0, 16, sign)) if a0 * c0 else v for a0, v in enumerate(row)]
        out.append(quad(row, sign))
    return out


def many_powers(first):
    out = [None, first]
    for k in range(2, 16):
        out.append(cmul(out[k // 2], out[k - k // 2]))
    return out


def lanes_at(step):
    return pl.ds(pl.multiple_of(step * 128, 128), 128)


def fwd_kernel(blocks, o0, o1, o2, o3, scratch):
    place = digits()
    block = 4 * place["x"] + place["y"]
    number = place["z"] * LOCAL + (8 * block + iota((8, 128), 0)) * 1024 + iota((8, 128), 1)
    forward = turn(128, NT, -1)

    def body(step, factor):
        lanes = lanes_at(step)
        y = sixteen([(blocks[t, 0:8, lanes], blocks[t, 8:16, lanes]) for t in range(16)], -1.0)
        factors = many_powers(factor)
        for c0 in range(4):
            slot = (c0 - place["z"]) & 3
            for c1 in range(4):
                value = y[c0][c1]
                if c0 + c1:
                    value = cmul(value, factors[c0 + 4 * c1])
                scratch[slot, c1, 0:8, lanes] = value[0]
                scratch[slot, c1, 8:16, lanes] = value[1]
        for j, out in enumerate((o0, o1, o2, o3)):
            out[:, :, lanes] = scratch[j, :, :, lanes]
        return cmul(factor, forward)

    lax.fori_loop(0, 8, body, phasor(number, NT, -1), unroll=4)


def mid_kernel(r0, r1, r2, r3, out):
    place = digits()
    block = 4 * place["x"] + place["y"]
    number = (8 * block + iota((8, 128), 0)) * 1024 + iota((8, 128), 1) + place["z"] * LOCAL
    forward = turn(128, 4 * LOCAL, -1)

    def body(step, factor):
        lanes = lanes_at(step)
        factors = powers(factor)
        for kk in range(4):
            x = [(r[kk, 0:8, lanes], r[kk, 8:16, lanes]) for r in (r0, r1, r2, r3)]
            for ka, value in enumerate(twist(quad(x, 1.0), factors)):
                out[4 * ka + kk, 0:8, lanes] = value[0]
                out[4 * ka + kk, 8:16, lanes] = value[1]
        return cmul(factor, forward)

    lax.fori_loop(0, 8, body, phasor(number, 4 * LOCAL, -1), unroll=4)


def spectrum_kernel(blocks, squares, disp, out, wide, work, back, rows_w, bins, flip, flat):
    hop, unhop = squares.at[0:2], squares.at[2:4]
    fwd_c, fwd_s, inv_c, inv_s = [squares.at[2 * k : 2 * k + 2] for k in range(2, 6)]
    for part in range(4):
        lanes = slice(256 * part, 256 * part + 256)
        wide[:, lanes] = dot_left([hop], [blocks[:, :, lanes].reshape(256, 256)])
    lane_f = powers(phasor(iota((8, 256), 1), 1024, -1))
    number = [256 * part + iota((8, 256), 1) for part in range(4)]
    cross_first = tuple(phasor(iota((8, 256), 0) * n, LOCAL, -1) for n in number)
    cross_step = [phasor(8 * n, LOCAL, -1) for n in number]

    def body(step, carry):
        rows, low_rows = eight(step * 8), eight(step * 8 + 128)
        x = []
        for part in range(4):
            lanes = slice(256 * part, 256 * part + 256)
            x.append(cmul((wide[rows, lanes], wide[low_rows, lanes]), carry[part]))
        y = twist(quad(x, -1.0), lane_f)
        for k in range(4):
            at = eight(step * 8 + 128 * k)
            work[at, 0:256] = y[k][0]
            work[at, 256:512] = y[k][1]
        return tuple(cmul(value, move) for value, move in zip(carry, cross_step))

    lax.fori_loop(0, 16, body, cross_first, unroll=4)
    bins[64:128, :] = jnp.zeros((64, 256), F32)
    for k in range(4):
        rows = slice(128 * k, 128 * k + 128)
        re, im = work[rows, 0:256], work[rows, 256:512]
        re, im = dot_right([re, -im], [fwd_c, fwd_s]), dot_right([re, im], [fwd_s, fwd_c])
        power = (re * re + im * im).reshape(16, 8, 256)
        bins[16 * k : 16 * k + 16, :] = jnp.sum(power, axis=1) * (1.0 / (NT * BIN_WIDTH))
        re, im = cmul((re, im), (disp[0, rows, :], disp[1, rows, :]))
        work[rows, 0:256] = re
        work[rows, 256:512] = im
    for half in range(2):
        flip[128 * half : 128 * half + 128, :] = bins[:, 128 * half : 128 * half + 128].T
    flat[...] = flip[pl.ds(0, 128, stride=2), :] + pltpu.roll(flip[pl.ds(1, 128, stride=2), :], 64, 1)
    for dest in range(16):
        out[dest, 128:136, :] = flat[8 * dest : 8 * dest + 8, :]
    re, im = work[:, 0:256], work[:, 256:512]
    back[0:256, :] = dot_left([inv_c, inv_s], [re, -im], NT_FORM)
    back[256:512, :] = dot_left([inv_s, inv_c], [re, im], NT_FORM)
    first = phasor(16 * iota((8, 128), 0), 1024, 1)
    forward, half_turn = turn(1, 1024, 1), turn(128, 1024, 1)
    freq = iota((8, 128), 1)
    cross_first = phasor(16 * iota((8, 128), 0) * freq, LOCAL, 1)
    cross_step, cross_half = phasor(freq, LOCAL, 1), phasor(128 * freq, LOCAL, 1)
    cross_part = powers(phasor(256 * freq, LOCAL, 1))

    def tail(a, carry):
        factor, other = carry
        for half in range(2):
            rows, low_rows = eight(a * 16 + 8 * half), eight(a * 16 + 8 * half + 256)
            x = [
                (back[rows, 128 * k : 128 * k + 128], back[low_rows, 128 * k : 128 * k + 128])
                for k in range(4)
            ]
            now = cmul(factor, half_turn) if half else factor
            after = cmul(other, cross_half) if half else other
            y = twist(quad(twist(x, powers(now)), 1.0), cross_part)
            for part in range(4):
                value = cmul(y[part], after)
                at = eight(a * 64 + part * 16 + 8 * half)
                rows_w[at, 0:128] = value[0]
                rows_w[at, 128:256] = value[1]
        return cmul(factor, forward), cmul(other, cross_step)

    lax.fori_loop(0, 16, tail, (first, cross_first), unroll=4)
    for part in range(4):
        got = dot_right([rows_w[256 * part : 256 * part + 256, :]], [unhop])
        for a in range(4):
            out[4 * part + a, 0:64, :] = got[64 * a : 64 * a + 64, 0:128]
            out[4 * part + a, 64:128, :] = got[64 * a : 64 * a + 64, 128:256]


def unmid_kernel(blocks, o0, o1, o2, o3):
    place = digits()
    outs = (o0, o1, o2, o3)
    total = blocks[0, 128:136, :]
    for k in range(1, 16):
        total = total + blocks[k, 128:136, :]
    for out in outs:
        out[520:528, :] = total
    block = 4 * place["x"] + place["y"]
    number = block + 16 * iota((8, 128), 0) + 1024 * iota((8, 128), 1) + place["z"] * LOCAL
    forward = turn(128, 4 * LOCAL, 1)

    def body(step, factor):
        rows, low_rows = eight(step * 8), eight(step * 8 + 64)
        factors = powers(factor)
        for kk in range(4):
            x = [(blocks[4 * ka + kk, rows, :], blocks[4 * ka + kk, low_rows, :]) for ka in range(4)]
            for out, value in zip(outs, quad(twist(x, factors), 1.0)):
                out[eight(step * 8 + 128 * kk), :] = value[0]
                out[eight(step * 8 + 128 * kk + 64), :] = value[1]
        return cmul(factor, forward)

    lax.fori_loop(0, 8, body, phasor(number, 4 * LOCAL, 1), unroll=4)
    pick = jnp.where(iota((16, 128), 1) == 0, 1.0, 0.0).astype(BF16)
    for j in range(4):
        high, low = halves(outs[(j + 1) % 4][0:512, :])
        row = lax.dot_general(pick, high, dims(NT_FORM), preferred_element_type=F32)
        row = row + lax.dot_general(pick, low, dims(NT_FORM), preferred_element_type=F32)
        for kk in range(4):
            outs[j][512 + kk : 513 + kk, :] = row[0:1, 128 * kk : 128 * kk + 128]
        outs[j][516:520, :] = jnp.zeros((4, 128), F32)


def unsixteen(x, factors):
    line = [None] * 16
    for c0 in range(4):
        for c1 in range(4):
            value = x[c0][c1]
            line[4 * c1 + c0] = cmul(value, factors[c0 + 4 * c1]) if c0 + c1 else value
    return sixteen(line, 1.0)


def inv_kernel(r0, r1, r2, r3, out, bins, blocks):
    place = digits()
    bins[...] = (r0[520:528, :] + r1[520:528, :]) + (r2[520:528, :] + r3[520:528, :])
    for s, value in enumerate((r0, r1, r2, r3)):
        blocks[(place["z"] - s) & 3] = value[0:520, :]
    block = 4 * place["x"] + place["y"]
    number = place["z"] * LOCAL + block + 16 * iota((8, 128), 0) + 1024 * iota((8, 128), 1)
    forward = turn(128, NT, 1)

    def body(step, factor):
        x = [
            [
                (blocks[c0, eight(step * 8 + 128 * c1), :], blocks[c0, eight(step * 8 + 128 * c1 + 64), :])
                for c1 in range(4)
            ]
            for c0 in range(4)
        ]
        y = unsixteen(x, many_powers(factor))
        for a0 in range(4):
            for a1 in range(4):
                out[4 * a1 + a0, eight(step * 8), :] = y[a0][a1][0]
                out[4 * a1 + a0, eight(step * 8 + 64), :] = y[a0][a1][1]
        return cmul(factor, forward)

    lax.fori_loop(0, 8, body, phasor(number, NT, 1), unroll=4)
    after = (place["z"] + 1) & 3
    lane = iota((8, 128), 1)
    factors = many_powers(phasor(after * LOCAL + block + 16 * (lane & 63), NT, 1))
    x = []
    for c0 in range(4):
        rows = [
            jnp.broadcast_to(blocks[c0, 512 + c1 : 513 + c1, :], (8, 128)) for c1 in range(4)
        ]
        x.append([(row, pltpu.roll(row, 64, 1)) for row in rows])
    y = unsixteen(x, factors)
    flat = []
    for t in range(16):
        re, im = y[t % 4][t // 4]
        flat.append(jnp.where(lane < 64, re, pltpu.roll(im, 64, 1)))
    wrap = after == 0
    for t in range(16):
        out[t, 128:136, :] = jnp.where(wrap, flat[(t + 1) % 16], flat[t])


def frames_kernel(blocks, mat, out_hbm, got, out, sems):
    columns = jnp.concatenate([blocks[a, 128:129, :] for a in range(16)], axis=0).T
    lane = iota((128, 128), 1)
    wave = phasor(16 * iota((64, 128), 0), W, 1)
    for a in range(16):
        here = blocks[a, 0:128, :]
        after = jnp.where(lane == 127, columns[:, a : a + 1], pltpu.roll(here, 127, 1))
        late = 0.5 + 0.5 * wave[0]
        early = 0.5 - 0.5 * wave[0]
        pieces = [here[0:64] * early, here[64:128] * early, after[0:64] * late, after[64:128] * late]
        got[a] = dot_left([mat], [jnp.concatenate(pieces, axis=0)])
        wave = cmul(wave, turn(1, W, 1))
    first = phasor(iota((8, 128), 0), W, -1)
    forward = turn(8, W, -1)

    def body(step, factor):
        rows, low_rows = eight(step * 8), eight(step * 8 + 128)
        factors = many_powers(factor)
        x = [(got[a, rows, :], got[a, low_rows, :]) for a in range(16)]
        y = sixteen([cmul(x[a], factors[a]) if a else x[a] for a in range(16)], -1.0)
        for c0 in range(4):
            for c1 in range(4):
                value = y[c0][c1]
                got[c0 + 4 * c1, rows, :] = (value[0] * value[0] + value[1] * value[1]) * (1.0 / W)
        return cmul(factor, forward)

    lax.fori_loop(0, 16, body, first, unroll=4)
    copies = []
    for c in range(16):
        out[:, 128 * c : 128 * c + 128] = got[c, 0:128, :].T
        if c % 4 == 3:
            lanes = pl.ds(128 * (c - 3), 512)
            copies.append(pltpu.make_async_copy(out.at[:, lanes], out_hbm.at[:, lanes], sems.at[c // 4]))
            copies[-1].start()
    for copy in copies:
        copy.wait()


def normal_kernel(b0, b1, b2, b3, out, side, pad):
    blocks = [b[...] for b in (b0, b1, b2, b3)]
    total = (blocks[0] + blocks[1]) + (blocks[2] + blocks[3])
    average = total * 0.25
    centred = [b - average for b in blocks]
    sq = [c * c for c in centred]
    variance = ((sq[0] + sq[1]) + (sq[2] + sq[3])) * 0.25
    spread = jnp.sqrt(jnp.maximum(variance, FLOOR_SHARE * average * average / BIN_WIDTH))
    grp = lax.axis_index("grp")
    for step in range(4):
        out[(grp - step) & 3] = centred[step] / spread
    at = digits()["z"] * 2
    pad[...] = jnp.zeros((128, 128), F32)
    for r in range(4):
        for half in range(2):
            pad[2 * r + half : 2 * r + half + 1, :] = out[r, pl.ds(at + half, 1), :] * 0.25
    flipped = pad[...].T
    for r in range(4):
        for half in range(2):
            column = flipped[:, 2 * r + half : 2 * r + half + 1]
            side[r, 128 * half : 128 * half + 128, :] = jnp.broadcast_to(column, (128, 128))


def correlation_kernel(side, c0, c1, c2, c3, out, cols):
    step = pl.program_id(0)

    @pl.when(step == 0)
    def _():
        place = digits()
        for s, value in enumerate((c0, c1, c2, c3)):
            cols[:, eight(((place["y"] - s) & 3) * 8), :] = value[...]

    for half in range(4):
        base = 32 * half
        factors = [[side[r, eight(step * 128 + base + g * 8), :] for r in range(4)] for g in range(4)]
        for k in range(32):
            line = [jnp.broadcast_to(cols[r, k : k + 1, :], (8, 128)) for r in range(4)]
            for g in range(4):
                total = (factors[g][0] * line[0] + factors[g][1] * line[1]) + (
                    factors[g][2] * line[2] + factors[g][3] * line[3]
                )
                at = base + 8 * g
                out[at : at + 8, 128 * k : 128 * k + 128] = total


def call(kernel, outs, scratch, *args, flops=1 << 20, specs=None, place=VMEM):
    size = sum(int(np.prod(s)) * 4 for s in outs)
    return pl.pallas_call(
        kernel,
        out_shape=[jax.ShapeDtypeStruct(s, F32) for s in outs],
        in_specs=specs or [VMEM] * len(args),
        out_specs=[place] * len(outs),
        scratch_shapes=[pltpu.VMEM(s, F32) if isinstance(s, tuple) else s for s in scratch],
        compiler_params=PARAMS,
        cost_estimate=pl.CostEstimate(flops=flops, bytes_accessed=2 * size, transcendentals=0),
    )(*args)


def ring(axis, step):
    stride = 1 << SHIFT[axis]
    pairs = []
    for device in range(64):
        digit = device // stride % 4
        pairs.append((device, device + ((digit + step) % 4 - digit) * stride))
    return pairs


def swap_z(blocks):
    moved = {step: lax.ppermute(blocks[step], "tm", ring("z", step)) for step in (2, 1, 3)}
    return [blocks[0], moved[1], moved[2], moved[3]]


def swap_plane(value):
    groups = [[16 * x + 4 * y + z for x in range(4) for y in range(4)] for z in range(4)]
    return lax.all_to_all(
        value, "tm", split_axis=0, concat_axis=0, axis_index_groups=groups, tiled=True
    )


FWD = (16, 16, 1024)


def on_device(seed_field):
    table = tables()
    tm = lax.axis_index("tm")

    seed = seed_field.reshape(2, HOPS, HOP)
    last = seed_field[0, :, LOCAL - TAPS :].reshape(8, 128)
    last = lax.ppermute(last, "tm", [(d, (d + 1) % 64) for d in range(64)]).reshape(2, TAPS)
    spots = (tm * LOCAL - TAPS + jnp.arange(TAPS, dtype=jnp.int32)) & (NT - 1)
    halo = ((last[0] + pulse_of(spots)) ** 2 + last[1] ** 2)[None, :]

    value = call(
        start_kernel, [FWD],
        [(136, 1024), (128, 1024), pltpu.VMEM((2, 768, 256), BF16), pltpu.SemaphoreType.DMA],
        seed, halo, table["toeplitz"], specs=[VMEM, VMEM, HBM],
    )[0]
    value = swap_plane(value)
    blocks = call(fwd_kernel, [(4, 16, 1024)] * 4, [(4, 4, 16, 1024)], value)
    *blocks, late = lax.optimization_barrier((*blocks, tm))
    row = lax.broadcasted_iota(jnp.int32, (512, 256), 0)
    number = (
        (late % 4 + 4 * (late // 4 % 4) + 16 * (late // 16))
        + 64 * (row & 127)
        + 8192 * (row >> 7)
        + 32768 * late
        + 32768 * (lax.broadcasted_iota(jnp.int32, (512, 256), 1) - late)
    )
    freq = jnp.where(number < NT // 2, number, number - NT)
    angle = (2.0 * math.pi / (1 << 28)) * (freq * freq & ((1 << 28) - 1)).astype(F32)
    disp = jnp.stack([jnp.cos(angle), jnp.sin(angle)])
    blocks = swap_z(blocks)
    *blocks, disp = lax.optimization_barrier((*blocks, disp))
    value = call(mid_kernel, [FWD], [], *blocks)[0]
    value = swap_plane(value)
    value = call(
        spectrum_kernel, [(16, 136, 128)],
        [(256, 1024), (512, 512), (512, 512), (1024, 256), (128, 256), (256, 128), (128, 128)],
        value, table["squares"], disp,
    )[0]
    value = swap_plane(value)
    blocks = call(unmid_kernel, [(528, 128)] * 4, [], value)
    blocks = swap_z(blocks)
    value, bins = call(inv_kernel, [(16, 136, 128), (8, 128)], [(4, 520, 128)], *blocks)
    value = swap_plane(value)

    alike = [bins] + [
        lax.ppermute(bins, "grp", [(g, (g + step) % 4) for g in range(4)]) for step in (1, 2, 3)
    ]
    normal, side = call(normal_kernel, [(4, 8, 128), (4, 256, 128)], [(128, 128)], *alike)
    columns = []
    for step in range(4):
        pairs = []
        for g in range(4):
            for d in range(64):
                x, y, z = d // 16, d // 4 % 4, d % 4
                pairs.append((g * 64 + d, x * 64 + g * 16 + (y + step) % 4 * 4 + z))
        columns.append(lax.ppermute(normal, ("grp", "tm"), pairs))

    spectrogram = call(
        frames_kernel, [(HOPS, W)], [(16, 256, 128), (HOPS, W), pltpu.SemaphoreType.DMA((4,))],
        value, table["frames"], place=HBM,
    )[0]
    spectrogram, side, *columns = lax.optimization_barrier((spectrogram, side, *columns))
    correlation = pl.pallas_call(
        correlation_kernel,
        grid=(2,),
        out_shape=jax.ShapeDtypeStruct((256, 4096), F32),
        in_specs=[pl.BlockSpec((4, 256, 128), lambda i: (0, 0, 0))]
        + [pl.BlockSpec((4, 8, 128), lambda i: (0, 0, 0))] * 4,
        out_specs=pl.BlockSpec((128, 4096), lambda i: (i, 0)),
        scratch_shapes=[pltpu.VMEM((4, 32, 128), F32)],
        compiler_params=PARAMS,
        cost_estimate=pl.CostEstimate(flops=1 << 23, bytes_accessed=1 << 22, transcendentals=0),
    )(side, *columns)
    return spectrogram[None], correlation


def solution(mesh):
    return jax.shard_map(
        on_device,
        mesh=mesh,
        in_specs=(P("grp", None, "tm"),),
        out_specs=(P("grp", "tm", None), P("tm", "grp")),
        check_vma=False,
    )
```
